256 devices in a mesh: gx: 8 (over z), gy: 32 (over x, y, core).
Axes of the slice: x: 4, y: 4, z: 8, core: 2. Of those that a mesh axis runs over, the one named last changes fastest.
Arguments:
- initial_field: float32 [8, 64, 8192], P(None, 'gx', 'gy'), may hold values from -6 to 6
- target_field: float32 [8, 64, 8192], P(None, 'gx', 'gy'), may hold values from -8 to 8
- land_mask: int32 [64, 8192], P('gx', 'gy'), may hold values 0 or 1
- conv_one: float32 [64, 73], replicated, may hold values from -0.75 to 0.75
- conv_two: float32 [64, 577], replicated, may hold values from -0.25 to 0.25
- head_weights: float32 [32, 65], replicated, may hold values from -0.75 to 0.75
- dir_one: float32 [64, 73], replicated, may hold values from -6 to 6
- dir_two: float32 [64, 577], replicated, may hold values from -6 to 6
- dir_three: float32 [32, 65], replicated, may hold values from -6 to 6
- group_ids: int32 [160], replicated, may hold values from 0 to 5, as said below
Outputs:
- final_field: float32 [8, 64, 8192], P(None, 'gx', 'gy')
- update_one: float32 [64, 73], replicated
- update_two: float32 [64, 577], replicated
- update_three: float32 [32, 65], replicated
The draws below stay inside these ranges and needn't reach their ends.
Inputs may be any that keep to these rules, and one draw needn't show every extreme that they name: `group_ids`: each of the 6 group numbers names 26 or 27 rows.
All inputs are finite; a program needn't handle non-finite values. No bound on the sum of `land_mask` on one device may be relied on, other than what follows from the above.
Results may differ from the reference program's by a relative error of at most 0.0024.
The reference program's roundings to bfloat16 on the way count: a program that leaves them out, or rounds other values in their place, can miss the bound.
Values may be sent and summed in bfloat16 or wider, within the bound.
No kernel may reach another device: no remote copies, remote signals or barrier semaphores. Data moves between devices by JAX's collectives and lax.ppermute only.
A program may use at most 64 MiB of HBM per device.

```python
import math
import jax
import jax.numpy as jnp
from jax import lax

LEV = 8
C = 64
K = 32
STEPS = 2
GROUPS = 6
NX = 64
NY = 8192
ROWS = 160
PARAMS = 43680


def draw_target_field(key, part):
    sample = jax.random.normal(key, (LEV, NX, NY), jnp.float32)
    position = jnp.arange(NX, dtype=jnp.float32)[None, :, None] / NX
    values = sample * 3.0 ** position
    return jnp.clip(values, -8.0, 8.0)


def draw_group_ids(key, part):
    return (jax.random.permutation(key, ROWS) % GROUPS).astype(jnp.int32)


def touch_ends(result, rng, low, largest):
    longest = result.shape.index(max(result.shape))
    spots = []
    for shift in (0, 1):
        where = [jax.random.randint(jax.random.fold_in(rng, axis), (), 0, length) for axis, length in enumerate(result.shape)]
        where[longest] = (where[longest] + shift) % result.shape[longest]
        spots.append(tuple(where))
    return result.at[spots[0]].set(low).at[spots[1]].set(largest)


def steps_of(key, shape, cuts, least, largest):
    gain, own = 1.0, jax.random.fold_in(key, 6)
    for dim, shards_of in cuts:
        steps = jnp.exp(jax.random.uniform(jax.random.fold_in(own, dim), (shards_of,), jnp.float32, least / len(cuts), largest / len(cuts)))
        gain = gain * jnp.repeat(steps, shape[dim] // shards_of).reshape([-1 if axis == dim else 1 for axis in range(len(shape))])
    return gain


def gaussian(key, extent, scale, limit, split=(), kind=jnp.bfloat16):
    entries = scale * jax.random.normal(key, extent, jnp.float32)
    if split:
        entries = entries * steps_of(key, extent, split, -0.22, 0.18)
    return jnp.clip(entries, -limit, limit).astype(kind)


def setup_inputs(seed: int = 0) -> dict:
    arg_keys = jax.random.split(jax.random.key(seed), 11)
    return {
        "initial_field": gaussian(arg_keys[0], (LEV, NX, NY), 1.0, 6.0, ((1, 8), (2, 32)), jnp.float32),
        "target_field": draw_target_field(jax.random.fold_in(arg_keys[10], 71), 0),
        "land_mask": touch_ends((jax.random.randint(arg_keys[2], (NX, NY), 0, 4) < 3).astype(jnp.int32), jax.random.fold_in(arg_keys[2], 1), 0, 1),
        "conv_one": gaussian(arg_keys[3], (C, 9 * LEV + 1), (9 * LEV) ** -0.5, 0.75, (), jnp.float32),
        "conv_two": gaussian(arg_keys[4], (C, 9 * C + 1), (9 * C) ** -0.5, 0.25, (), jnp.float32),
        "head_weights": gaussian(arg_keys[5], (K, C + 1), C ** -0.5, 0.75, (), jnp.float32),
        "dir_one": gaussian(arg_keys[6], (C, 9 * LEV + 1), 1.0, 6.0, (), jnp.float32),
        "dir_two": gaussian(arg_keys[7], (C, 9 * C + 1), 1.0, 6.0, (), jnp.float32),
        "dir_three": gaussian(arg_keys[8], (K, C + 1), 1.0, 6.0, (), jnp.float32),
        "group_ids": draw_group_ids(jax.random.fold_in(arg_keys[10], 71), 0),
    }


OFFSETS = ((0, 0), (0, 1), (0, 2), (1, 0), (1, 1), (1, 2), (2, 0), (2, 1), (2, 2))
CONTRACT_ROWS = (((1,), (1,)), ((), ()))
CONTRACT_COLS = (((0,), (0,)), ((), ()))

def silu_parts(activation):
    logistic = jax.nn.sigmoid(activation)
    return (activation * logistic, logistic * (1.0 + activation * (1.0 - logistic)))

def convolve(padded, kernel, bias_column):
    inputs = padded.shape[0]
    height = padded.shape[1] - 2
    breadth = padded.shape[2] - 2
    summed = jnp.zeros((kernel.shape[0], height * breadth), jnp.float32)
    for offset_index, offset_pair in enumerate(OFFSETS):
        row_start, col_start = offset_pair
        window = padded[:, row_start:row_start + height, col_start:col_start + breadth].reshape(inputs, height * breadth)
        weight_block = kernel[:, offset_index * inputs:(offset_index + 1) * inputs]
        summed = summed + jnp.dot(weight_block, window, preferred_element_type=jnp.float32)
    return summed.reshape(-1, height, breadth) + bias_column[:, None, None]

def convolve_back(padded, kernel, errors, precision):
    inputs = padded.shape[0]
    height = padded.shape[1] - 2
    breadth = padded.shape[2] - 2
    flat_error = errors.reshape(errors.shape[0], height * breadth)
    pieces = []
    input_grad = jnp.zeros(padded.shape, jnp.float32)
    for offset_index, offset_pair in enumerate(OFFSETS):
        row_start, col_start = offset_pair
        window = padded[:, row_start:row_start + height, col_start:col_start + breadth].reshape(inputs, height * breadth)
        pieces.append(lax.dot_general(flat_error, window, CONTRACT_ROWS, precision=precision, preferred_element_type=jnp.float32))
        weight_block = kernel[:, offset_index * inputs:(offset_index + 1) * inputs]
        carried = lax.dot_general(weight_block, flat_error, CONTRACT_COLS, precision=precision, preferred_element_type=jnp.float32)
        input_grad = input_grad.at[:, row_start:row_start + height, col_start:col_start + breadth].add(carried.reshape(inputs, height, breadth))
    return (jnp.concatenate(pieces, axis=1), input_grad)

def neighbours(padded):
    return (padded[:, 2:, 1:-1], padded[:, :-2, 1:-1], padded[:, 1:-1, 2:], padded[:, 1:-1, :-2])

def advance(padded, coeffs, wet_cells):
    center = padded[:, 1:-1, 1:-1]
    change = jnp.zeros(center.shape, jnp.float32)
    for direction, beside in enumerate(neighbours(padded)):
        change = change + coeffs[direction] * (beside - center)
    return center + wet_cells * change

def advance_back(padded, coeffs, wet_cells, adjoint):
    center = padded[:, 1:-1, 1:-1]
    weighted = wet_cells * adjoint
    grad_coeffs = []
    remains = adjoint
    for direction, beside in enumerate(neighbours(padded)):
        grad_coeffs.append(weighted * (beside - center))
        remains = remains - weighted * coeffs[direction]
    carried = weighted * coeffs
    grad_pad = jnp.zeros(padded.shape, jnp.float32)
    grad_pad = grad_pad.at[:, 2:, 1:-1].add(carried[0])
    grad_pad = grad_pad.at[:, :-2, 1:-1].add(carried[1])
    grad_pad = grad_pad.at[:, 1:-1, 2:].add(carried[2])
    grad_pad = grad_pad.at[:, 1:-1, :-2].add(carried[3])
    grad_pad = grad_pad.at[:, 1:-1, 1:-1].add(remains)
    return (jnp.stack(grad_coeffs), grad_pad)

def split_kernels(conv_one, conv_two, head_weights):
    return [(weights[:, :-1].astype(jnp.bfloat16), weights[:, -1]) for weights in (conv_one, conv_two, head_weights)]

def tail_forward(hidden_pad, kernels):
    second_pre = convolve(hidden_pad, kernels[1][0], kernels[1][1])
    second_out = silu_parts(second_pre)[0].astype(jnp.bfloat16)
    channels = second_out.shape[0]
    height = second_out.shape[1]
    breadth = second_out.shape[2]
    head_pre = jnp.dot(kernels[2][0], second_out.reshape(channels, height * breadth), preferred_element_type=jnp.float32) + kernels[2][1][:, None]
    logistic = jax.nn.sigmoid(head_pre)
    coeffs = (0.25 * logistic).reshape(4, -1, height, breadth)
    return (second_pre, second_out, logistic, coeffs)

def tail_back(hidden_pad, kernels, stored_tail, grad_coeffs):
    second_pre, second_out, logistic, coeffs = stored_tail
    head_error = grad_coeffs.reshape(logistic.shape) * (0.25 * logistic * (1.0 - logistic))
    head_round = head_error.astype(jnp.bfloat16)
    flat_out = second_out.reshape(second_out.shape[0], -1)
    head_grad = jnp.concatenate([lax.dot_general(head_round, flat_out, CONTRACT_ROWS, preferred_element_type=jnp.float32), lax.optimization_barrier(jnp.sum(head_error, axis=1))[:, None]], axis=1)
    hidden_back = lax.dot_general(kernels[2][0], head_round, CONTRACT_COLS, preferred_element_type=jnp.float32)
    second_error = hidden_back.reshape(second_pre.shape) * silu_parts(second_pre)[1]
    weight_grad, hidden_grad = convolve_back(hidden_pad, kernels[1][0], second_error.astype(jnp.bfloat16), None)
    second_grad = jnp.concatenate([weight_grad, lax.optimization_barrier(jnp.sum(second_error, axis=(1, 2)))[:, None]], axis=1)
    return (head_grad, second_grad, hidden_grad)

def first_back(tracer_round, kernel, first_error):
    first_round = first_error.astype(jnp.bfloat16)
    weight_grad, tracer_grad = convolve_back(tracer_round, kernel, first_round, None)
    return (jnp.concatenate([weight_grad, lax.optimization_barrier(jnp.sum(first_error, axis=(1, 2)))[:, None]], axis=1), tracer_grad)

def finish(gradients, directions, group_ids):
    norm_total = jnp.zeros((), jnp.float32)
    for member in gradients:
        norm_total = norm_total + jnp.sum(member * member)
    factor = 1.0 / jnp.maximum(jnp.sqrt(norm_total), 1.0)
    clipped = [member * factor for member in gradients]
    clip_rows = jnp.concatenate([lax.optimization_barrier(jnp.sum(member * member, axis=1)) for member in clipped])
    dir_rows = jnp.concatenate([lax.optimization_barrier(jnp.sum(member * member, axis=1)) for member in directions])
    choose = (group_ids[:, None] == jnp.arange(GROUPS, dtype=jnp.int32)[None, :]).astype(jnp.float32)
    ratios = jnp.sqrt(lax.optimization_barrier(jnp.sum(choose * clip_rows[:, None], axis=0))) / jnp.sqrt(lax.optimization_barrier(jnp.sum(choose * dir_rows[:, None], axis=0)) + 1e-06)
    row_ratio = lax.optimization_barrier(jnp.sum(choose * ratios[None, :], axis=1))
    scaling = math.sqrt(PARAMS)
    outputs = []
    row_start = 0
    for member, heading in zip(clipped, directions):
        row_count = member.shape[0]
        outputs.append(scaling * (member + row_ratio[row_start:row_start + row_count, None] * heading))
        row_start = row_start + row_count
    return outputs

def step_forward(tracer, kernels, wet_cells):
    tracer_pad = jnp.pad(tracer, ((0, 0), (1, 1), (1, 1)))
    tracer_round = tracer_pad.astype(jnp.bfloat16)
    first_pre = convolve(tracer_round, kernels[0][0], kernels[0][1])
    hidden = silu_parts(first_pre)[0].astype(jnp.bfloat16)
    hidden_pad = jnp.pad(hidden, ((0, 0), (1, 1), (1, 1)))
    stored_tail = tail_forward(hidden_pad, kernels)
    return (advance(tracer_pad, stored_tail[3], wet_cells), (tracer_pad, tracer_round, first_pre, hidden_pad, stored_tail))

def reference(initial_field, target_field, land_mask, conv_one, conv_two, head_weights, dir_one, dir_two, dir_three, group_ids):
    wet_cells = land_mask.astype(jnp.float32)
    kernels = split_kernels(conv_one, conv_two, head_weights)
    tracer = wet_cells * initial_field
    history = [tracer]
    for step_index in range(STEPS):
        tracer = step_forward(tracer, kernels, wet_cells)[0]
        history.append(tracer)
    final_field = tracer
    adjoint = wet_cells * (tracer - target_field)
    totals = [jnp.zeros(conv_one.shape, jnp.float32), jnp.zeros(conv_two.shape, jnp.float32), jnp.zeros(head_weights.shape, jnp.float32)]
    for step_index in reversed(range(STEPS)):
        stored = step_forward(history[step_index], kernels, wet_cells)[1]
        tracer_pad, tracer_round, first_pre, hidden_pad, stored_tail = stored
        grad_coeffs, near_grad = advance_back(tracer_pad, stored_tail[3], wet_cells, adjoint)
        head_grad, second_grad, hidden_grad = tail_back(hidden_pad, kernels, stored_tail, grad_coeffs)
        first_error = hidden_grad[:, 1:-1, 1:-1] * silu_parts(first_pre)[1]
        first_grad, conv_grad = first_back(tracer_round, kernels[0][0], first_error)
        adjoint = (conv_grad + near_grad)[:, 1:-1, 1:-1]
        totals = [totals[0] + first_grad, totals[1] + second_grad, totals[2] + head_grad]
    updates = finish(totals, [dir_one, dir_two, dir_three], group_ids)
    return (final_field, updates[0], updates[1], updates[2])
```

```python
import math

import jax
import jax.numpy as jnp
from jax import lax
from jax.experimental import pallas as pl
from jax.experimental.pallas import tpu as pltpu
from jax.sharding import Mesh
from jax.sharding import PartitionSpec as P

LEV = 8
C = 64
K = 32
GROUPS = 6
PARAMS = 43680
GY = ("gy_0", "gy_1", "gy_2")
H = 8
W = 256
PITCH = 384
REACH = 6
BF = jnp.bfloat16
F32 = jnp.float32
NT = (((1,), (1,)), ((), ()))


def dot(a, b):
    return jnp.dot(a, b, preferred_element_type=F32)


def dot_nt(a, b):
    return lax.dot_general(a, b, NT, preferred_element_type=F32)


def turned(v, by):
    return pltpu.roll(v, by % v.shape[1], 1)


def sigmoid(v):
    return 0.5 * jnp.tanh(0.5 * v) + 0.5


def silu_slope(v, s):
    return s * (1.0 + v * (1.0 - s))


def pack_rows(init_ref, target_ref, mask_ref, low_ref, high_ref):
    wet = mask_ref[...].astype(F32)
    low_ref[64:72, :] = wet
    high_ref[64:72, :] = wet
    for k in range(REACH):
        low_ref[k * 8 : k * 8 + 8, :] = init_ref[:, k, :] * wet[k : k + 1]
        r = H - REACH + k
        high_ref[k * 8 : k * 8 + 8, :] = init_ref[:, r, :] * wet[r : r + 1]
    for k in range(2):
        low_ref[48 + k * 8 : 56 + k * 8, :] = target_ref[:, k, :]
        high_ref[48 + k * 8 : 56 + k * 8, :] = target_ref[:, H - 2 + k, :]


def row_parts(r, init_ref, target_ref, mask_ref, below_ref, above_ref):
    if 0 <= r < H:
        wet = mask_ref[r : r + 1, :].astype(F32)
        return init_ref[:, r, :] * wet, wet, target_ref[:, r, :]
    ref, k = (below_ref, r + REACH) if r < 0 else (above_ref, r - H)
    field = ref[k * 8 : k * 8 + 8, :]
    m = r + H if r < 0 else r - H
    wet = ref[64 + m : 65 + m, :]
    target = None
    if -2 <= r < H + 2:
        t = r + 2 if r < 0 else r - H
        target = ref[48 + 8 * t : 56 + 8 * t, :]
    return field, wet, target


def pack_cols(init_ref, target_ref, mask_ref, below_ref, above_ref, left_ref, right_ref):
    lane = lax.broadcasted_iota(jnp.int32, (8, 128), 1)
    for r in range(-REACH, H + REACH):
        field, wet, target = row_parts(r, init_ref, target_ref, mask_ref, below_ref, above_ref)
        wet = jnp.broadcast_to(wet, (8, W))
        a = jnp.where(lane < 32, field[:, :128], turned(wet[:, :128], 32))
        b = jnp.where(lane >= 96, field[:, 128:], turned(wet[:, 128:], -32))
        if target is not None:
            a = jnp.where(lane < 64, a, turned(target[:, :128], 64))
            b = jnp.where(lane >= 64, b, turned(target[:, 128:], -64))
        at = (r + REACH) * 8
        left_ref[at : at + 8, :] = a
        right_ref[at : at + 8, :] = b


def prepare(one_ref, two_ref, head_ref, w1_ref, w2_ref, w3_ref, w3t_ref, w2t_ref, w1t_ref, bias_ref):
    one, two, head = one_ref[...], two_ref[...], head_ref[...]
    w1_ref[...] = one[:, : 9 * LEV].astype(BF)
    w2_ref[...] = two[:, : 9 * C].astype(BF)
    w3_ref[...] = head[:, :C].astype(BF)
    w3t_ref[...] = head[:, :C].T.astype(BF)
    w2t_ref[...] = jnp.concatenate(
        [two[:, (8 - k) * C : (9 - k) * C].T for k in range(9)], axis=1
    ).astype(BF)
    w1t_ref[...] = jnp.concatenate(
        [
            jnp.concatenate(
                [one[:, (3 * (2 - a) + b) * LEV : (3 * (2 - a) + b + 1) * LEV].T for a in range(3)],
                axis=1,
            )
            for b in range(3)
        ],
        axis=0,
    ).astype(BF)
    bias_ref[0:64, :] = jnp.broadcast_to(one[:, 9 * LEV :], (64, 128))
    bias_ref[64:128, :] = jnp.broadcast_to(two[:, 9 * C :], (64, 128))
    bias_ref[128:160, :] = jnp.broadcast_to(head[:, C:], (32, 128))


def lanes(parts):
    return parts[0] if len(parts) == 1 else jnp.concatenate(parts, axis=1)


def cut(v, n):
    return [v[:, k * PITCH : (k + 1) * PITCH] for k in range(n)]


def folded(v):
    total = v[:, :128]
    for k in range(1, v.shape[1] // 128):
        total = total + v[:, k * 128 : (k + 1) * 128]
    return total


def main(
    place_ref, init_ref, target_ref, mask_ref, below_ref, above_ref, fromleft_ref, fromright_ref,
    w1_ref, w2_ref, w3_ref, w3t_ref, w2t_ref, w1t_ref, bias_ref,
    final_ref, grad_ref,
    xc0, xc1, wet_s, tgt, hc0, hc1, h2s, sp10, sp11, sp2, wd, ec0, ec1, e1s, rem, up, down, fin,
    b1g, b2g, b3g, g1, g2, g3,
):
    lane = lax.broadcasted_iota(jnp.int32, (8, 128), 1)
    zero = jnp.zeros((8, 128), F32)
    for r in range(-REACH, H + REACH):
        field, wet, target = row_parts(r, init_ref, target_ref, mask_ref, below_ref, above_ref)
        at = (r + REACH) * 8
        fl, fr = fromleft_ref[at : at + 8, :], fromright_ref[at : at + 8, :]

        def rim(by):
            right, left = (turned(fr, -by), turned(fl, by)) if by else (fr, fl)
            return jnp.where(lane < 16, right, jnp.where(lane >= 112, left, zero))

        row = jnp.concatenate([field, rim(0)], axis=1)
        xc0[at * 3 : at * 3 + 24, :] = jnp.concatenate(
            [turned(row, 1), row, turned(row, -1)], axis=0
        )
        wet_s[at : at + 8, :] = jnp.concatenate([jnp.broadcast_to(wet, (8, W)), rim(32)], axis=1)
        if target is not None:
            tgt[at : at + 8, :] = jnp.concatenate([target, rim(64)], axis=1)
    for ref in (b1g, b2g, b3g, g1, g2, g3):
        ref[...] = jnp.zeros(ref.shape, F32)
    for r in (4, 5, 14, 15):
        ec0[r * 192 : r * 192 + 192, :] = jnp.zeros((192, PITCH), BF)

    col = lax.broadcasted_iota(jnp.int32, (1, PITCH), 1)
    col = jnp.where(col < 320, col, col - PITCH) + place_ref[1]
    col_in = jnp.where((col >= 0) & (col < place_ref[3]), 1.0, 0.0).astype(F32)

    def inside(r):
        i = place_ref[0] + r - REACH
        return col_in * jnp.where((i >= 0) & (i < place_ref[2]), 1.0, 0.0)

    def bias(at, n, times=1):
        b = bias_ref[at : at + n, :]
        return jnp.concatenate([b] * (3 * times), axis=1)

    def part(ref, r, size, first=0, count=None):
        start = r * size + first
        if not isinstance(start, int):
            start = pl.multiple_of(start, 8 if size % 16 or first % 16 else 16)
        return ref.at[pl.ds(start, size if count is None else count), :]

    def loop(lo, hi, per, body):
        def step(i, carry):
            body([lo + REACH + i * per + k for k in range(per)])
            return carry

        lax.fori_loop(0, (hi - lo) // per, step, 0)

    def thrice(v):
        return turned(v, 1), v, turned(v, -1)

    def store_thrice(ref, r, v):
        for k, piece in enumerate(thrice(v)):
            part(ref, r, 192, 64 * k, 64)[...] = piece.astype(BF)

    def first_layer(xc, hc, sp1):
        def body(rs):
            x9 = lanes([part(xc, r - 1, 24, 0, 72)[...].astype(BF) for r in rs])
            for r, z in zip(rs, cut(dot(w1_ref[...], x9), len(rs))):
                z = z + bias(0, 64)
                s = sigmoid(z)
                keep = inside(r)
                store_thrice(hc, r, z * s * keep)
                part(sp1, r, 64)[...] = silu_slope(z, s) * keep

        return body

    def second_layer(hc, rs):
        z = dot(w2_ref[...], lanes([part(hc, r - 1, 192, 0, 576)[...] for r in rs]))
        z = z + bias(64, 64, len(rs))
        s = sigmoid(z)
        h2 = (z * s).astype(BF)
        q = dot(w3_ref[...], h2) + bias(128, 32, len(rs))
        return h2, silu_slope(z, s), sigmoid(q)

    def slopes(xc, r):
        x = part(xc, r, 24, 8, 8)[...]
        beside = (
            part(xc, r + 1, 24, 8, 8)[...],
            part(xc, r - 1, 24, 8, 8)[...],
            part(xc, r, 24, 16, 8)[...],
            part(xc, r, 24, 0, 8)[...],
        )
        return x, [b - x for b in beside]

    def tail_zero(rs):
        h2, slope, p = second_layer(hc0, rs)
        n = len(rs)
        for r, h2r, sr, pr in zip(rs, cut(h2, n), cut(slope, n), cut(p, n)):
            part(h2s, r, 64)[...] = h2r
            part(sp2, r, 64)[...] = sr
            x, diff = slopes(xc0, r)
            wet = part(wet_s, r, 8)[...]
            change = jnp.zeros_like(x)
            for k in range(4):
                pk = pr[8 * k : 8 * k + 8]
                move = 0.25 * pk * diff[k]
                change = change + move
                part(wd, r, 32, 8 * k, 8)[...] = wet * move * (1.0 - pk)
            for k, piece in enumerate(thrice(x + wet * change)):
                part(xc1, r, 24, 8 * k, 8)[...] = piece

    def tail_grads(rs, e3, e2, h2, hc):
        b3g[...] += sum(folded(e[:, :W]) for e in e3)
        b2g[...] += sum(folded(e[:, :W]) for e in e2)
        g3[...] += dot_nt(
            lanes([e[:, :W].astype(BF) for e in e3]), lanes([v[:, :W] for v in h2])
        )
        g2[...] += dot_nt(
            lanes([e[:, :W].astype(BF) for e in e2]),
            lanes([part(hc, r - 1, 192, 0, 576)[:, :W] for r in rs]),
        )

    def tail_one(own):
        def body(rs):
            h2, slope, p = second_layer(hc1, rs)
            n = len(rs)
            e3s = []
            for r, pr in zip(rs, cut(p, n)):
                x, diff = slopes(xc1, r)
                wet = part(wet_s, r, 8)[...]
                c = [0.25 * pr[8 * k : 8 * k + 8] for k in range(4)]
                move = [c[k] * diff[k] for k in range(4)]
                new = x + wet * (move[0] + move[1] + move[2] + move[3])
                if own:
                    part(fin, r, 8)[...] = new
                g = wet * (new - part(tgt, r, 8)[...])
                wg = wet * g
                t = [wg * c[k] for k in range(4)]
                left = g - t[0] - t[1] - t[2] - t[3]
                part(rem, r, 8)[...] = left + turned(t[2], 1) + turned(t[3], -1)
                part(up, r, 8)[...] = t[0]
                part(down, r, 8)[...] = t[1]
                e3s.append(
                    jnp.concatenate(
                        [wg * move[k] * (1.0 - pr[8 * k : 8 * k + 8]) for k in range(4)], axis=0
                    )
                )
            e2 = dot(w3t_ref[...], lanes([e.astype(BF) for e in e3s])) * slope
            e2s = cut(e2, n)
            for r, e in zip(rs, e2s):
                store_thrice(ec1, r, e)
            if own:
                tail_grads(rs, e3s, e2s, cut(h2, n), hc1)

        return body

    def first_error(ec, sp1, rs):
        e = dot(w2t_ref[...], lanes([part(ec, r - 1, 192, 0, 576)[...] for r in rs]))
        return [v * part(sp1, r, 64)[...] for r, v in zip(rs, cut(e, len(rs)))]

    def first_grads(rs, e1, xc, width):
        b1g[...] += sum(folded(e[:, :width]) for e in e1)
        g1[...] += dot_nt(
            lanes([e[:, :width].astype(BF) for e in e1]),
            lanes([part(xc, r - 1, 24, 0, 72)[:, :width].astype(BF) for r in rs]),
        )

    def first_one(own):
        def body(rs):
            e1 = first_error(ec1, sp11, rs)
            for r, e in zip(rs, e1):
                part(e1s, r, 64)[...] = e.astype(BF)
            if own:
                first_grads(rs, e1, xc1, W)

        return body

    def back_zero(rs):
        y = dot(w1t_ref[...], lanes([part(e1s, r - 1, 64, 0, 192)[...] for r in rs]))
        e3s = []
        for r, yr in zip(rs, cut(y, len(rs))):
            g = part(rem, r, 8)[...] + part(up, r - 1, 8)[...] + part(down, r + 1, 8)[...]
            g = g + yr[8:16] + turned(yr[0:8], -1) + turned(yr[16:24], 1)
            e3 = jnp.concatenate([g] * 4, axis=0) * part(wd, r, 32)[...]
            e3s.append(jnp.concatenate([e3[:, :W], jnp.zeros((K, PITCH - W), F32)], axis=1))
        e2 = dot(w3t_ref[...], lanes([e.astype(BF) for e in e3s]))
        e2s = [v * part(sp2, r, 64)[...] for r, v in zip(rs, cut(e2, len(rs)))]
        for r, e in zip(rs, e2s):
            store_thrice(ec0, r, e)
        tail_grads(rs, e3s, e2s, [part(h2s, r, 64)[...] for r in rs], hc0)

    def first_zero(rs):
        first_grads(rs, first_error(ec0, sp10, rs), xc0, PITCH)

    loop(-5, 13, 2, first_layer(xc0, hc0, sp10))
    loop(-4, 12, 2, tail_zero)
    loop(-3, 11, 2, first_layer(xc1, hc1, sp11))
    tail_one(False)([4, 5])
    tail_one(False)([14, 15])
    loop(0, 8, 2, tail_one(True))
    first_one(False)([5, 14])
    loop(0, 8, 2, first_one(True))
    loop(0, 8, 2, back_zero)
    loop(-1, 9, 2, first_zero)

    for r in range(H):
        final_ref[:, r, :] = fin[(r + REACH) * 8 : (r + REACH) * 8 + 8, :W]
    for k in range(4):
        grad_ref[k * 64 : k * 64 + 64, :] = g2[:, k * 128 : k * 128 + 128]
    grad_ref[256:320, :] = jnp.concatenate([g2[:, 512:576], g1[:, 0:64]], axis=1)
    sums = [jnp.sum(ref[...], axis=1, keepdims=True) for ref in (b1g, b2g, b3g)]
    sums[2] = jnp.concatenate([sums[2], jnp.zeros((32, 1), F32)], axis=0)
    grad_ref[320:384, :] = jnp.concatenate(
        [
            g1[:, 64:72],
            *sums,
            jnp.zeros((64, 53), F32),
            jnp.concatenate([g3[...], jnp.zeros((32, 64), F32)], axis=0),
        ],
        axis=1,
    )


def finish(total_ref, d1_ref, d2_ref, d3_ref, gid_ref, u1_ref, u2_ref, u3_ref):
    t = [total_ref[k * 64 : k * 64 + 64, :] for k in range(6)]
    two = jnp.concatenate([*t[:4], t[4][:, :64], t[5][:, 9:10]], axis=1)
    one = jnp.concatenate([t[4][:, 64:], t[5][:, :8], t[5][:, 8:9]], axis=1)
    three = jnp.concatenate([t[5][:32, 64:], t[5][:32, 10:11]], axis=1)

    def row_sums(parts):
        return jnp.concatenate([jnp.sum(v * v, axis=1, keepdims=True) for v in parts], axis=0)

    grads = (one, two, three)
    dirs = (d1_ref[...], d2_ref[...], d3_ref[...])
    norm = jnp.sqrt(jnp.sum(row_sums(grads), axis=0, keepdims=True))
    factor = 1.0 / jnp.maximum(norm, 1.0)
    clipped = [v * factor for v in grads]
    group = lax.broadcasted_iota(jnp.int32, (160, 128), 1)
    choose = jnp.where(gid_ref[...] == group, 1.0, 0.0)
    clip_groups = jnp.sum(choose * row_sums(clipped), axis=0, keepdims=True)
    dir_groups = jnp.sum(choose * row_sums(dirs), axis=0, keepdims=True)
    ratios = jnp.sqrt(clip_groups) / jnp.sqrt(dir_groups + 1e-06)
    row_ratio = jnp.sum(choose * ratios, axis=1, keepdims=True)
    scaling = math.sqrt(PARAMS)
    at = 0
    for ref, v, d in zip((u1_ref, u2_ref, u3_ref), clipped, dirs):
        n = v.shape[0]
        ref[...] = scaling * (v + row_ratio[at : at + n] * d)
        at += n


def shape(dims, dtype=F32):
    return jax.ShapeDtypeStruct(dims, dtype)


def kernel(body, outs, cost, **more):
    return pl.pallas_call(
        body,
        out_shape=outs,
        cost_estimate=pl.CostEstimate(flops=cost, bytes_accessed=cost, transcendentals=0),
        compiler_params=pltpu.CompilerParams(vmem_limit_bytes=60 * 2**20),
        **more,
    )


def exchange(forward, backward, axis):
    count = lax.axis_size(axis)
    ahead = [(i, i + 1) for i in range(count - 1)]
    back = [(b, a) for a, b in ahead]
    return lax.ppermute(forward, axis, ahead), lax.ppermute(backward, axis, back)


def total_of(grad):
    near, far = ("gy_0", "gy_1"), ("gx", "gy_2")
    n = lax.axis_size(near)
    pieces = grad.reshape(n, -1, 128)
    own = jnp.sum(lax.all_to_all(pieces, near, 0, 0, tiled=True), axis=0)
    m = lax.axis_size(far)
    copies = jnp.broadcast_to(own, (m, *own.shape))
    own = jnp.sum(lax.all_to_all(copies, far, 0, 0, tiled=True), axis=0)
    copies = jnp.broadcast_to(own, (n, *own.shape))
    return lax.all_to_all(copies, near, 0, 0, tiled=True).reshape(grad.shape)


def per_device(init, target, mask, one, two, head, d1, d2, d3, gid):
    place = jnp.stack(
        [
            lax.axis_index("gx") * H,
            lax.axis_index(GY) * W,
            lax.axis_size("gx") * H,
            lax.axis_size(GY) * W,
        ]
    ).astype(jnp.int32)
    to_low, to_high = kernel(pack_rows, [shape((72, W))] * 2, 10**5)(init, target, mask)
    below, above = exchange(to_high, to_low, "gx")
    weights = kernel(
        prepare,
        [
            shape((C, 72), BF), shape((C, 576), BF), shape((K, C), BF), shape((C, K), BF),
            shape((C, 576), BF), shape((24, 192), BF), shape((160, 128)),
        ],
        10**6,
    )(one, two, head)
    to_left, to_right = kernel(pack_cols, [shape((160, 128))] * 2, 10**5)(
        init, target, mask, below, above
    )
    from_left, from_right = exchange(to_right, to_left, GY)

    def rows(size, dtype=F32):
        return pltpu.VMEM((20 * size, PITCH), dtype)

    vmem = pl.BlockSpec(memory_space=pltpu.VMEM)
    final, grad = kernel(
        main,
        [shape((LEV, H, W)), shape((384, 128))],
        10**7,
        in_specs=[pl.BlockSpec(memory_space=pltpu.SMEM)] + [vmem] * 14,
        out_specs=[vmem] * 2,
        scratch_shapes=[
            rows(24), rows(24), rows(8), rows(8), rows(192, BF), rows(192, BF), rows(64, BF),
            rows(64), rows(64), rows(64), rows(32), rows(192, BF), rows(192, BF), rows(64, BF),
            rows(8), rows(8), rows(8), rows(8),
            pltpu.VMEM((64, 128), F32), pltpu.VMEM((64, 128), F32), pltpu.VMEM((32, 128), F32),
            pltpu.VMEM((64, 72), F32), pltpu.VMEM((64, 576), F32), pltpu.VMEM((32, 64), F32),
        ],
    )(place, init, target, mask, below, above, from_left, from_right, *weights)
    total = total_of(grad)
    u1, u2, u3 = kernel(finish, [shape(one.shape), shape(two.shape), shape(head.shape)], 10**6)(
        total, d1, d2, d3, gid.reshape(-1, 1)
    )
    return final, u1, u2, u3


def solution(mesh):
    count = mesh.shape["gy"] // 8
    torus = Mesh(mesh.devices.reshape(mesh.shape["gx"], count, 4, 2), ("gx", *GY))
    placed = (P(None, "gx", GY), P(None, "gx", GY), P("gx", GY), P(), P(), P(), P(), P(), P(), P())
    return jax.shard_map(
        per_device,
        mesh=torus,
        in_specs=placed,
        out_specs=(P(None, "gx", GY), P(), P(), P()),
        check_vma=False,
    )
```

```python
import math

import jax
import jax.numpy as jnp
from jax import lax
from jax.experimental import pallas as pl
from jax.experimental.pallas import tpu as pltpu
from jax.sharding import Mesh
from jax.sharding import PartitionSpec as P

LEV = 8
C = 64
K = 32
GROUPS = 6
PARAMS = 43680
GY = ("gy_0", "gy_1", "gy_2")
H = 8
W = 256
PITCH = 384
REACH = 6
BF = jnp.bfloat16
F32 = jnp.float32
NT = (((1,), (1,)), ((), ()))


def dot(a, b):
    return jnp.dot(a, b, preferred_element_type=F32)


def dot_nt(a, b):
    return lax.dot_general(a, b, NT, preferred_element_type=F32)


def turned(v, by):
    return pltpu.roll(v, by % v.shape[1], 1)


def sigmoid(v):
    return 0.5 * jnp.tanh(0.5 * v) + 0.5


def silu_slope(v, s):
    return s * (1.0 + v * (1.0 - s))


def pack_rows(init_ref, target_ref, mask_ref, low_ref, high_ref):
    wet = mask_ref[...].astype(F32)
    low_ref[64:72, :] = wet
    high_ref[64:72, :] = wet
    for k in range(REACH):
        low_ref[k * 8 : k * 8 + 8, :] = init_ref[:, k, :] * wet[k : k + 1]
        r = H - REACH + k
        high_ref[k * 8 : k * 8 + 8, :] = init_ref[:, r, :] * wet[r : r + 1]
    for k in range(2):
        low_ref[48 + k * 8 : 56 + k * 8, :] = target_ref[:, k, :]
        high_ref[48 + k * 8 : 56 + k * 8, :] = target_ref[:, H - 2 + k, :]


def row_parts(r, init_ref, target_ref, mask_ref, below_ref, above_ref):
    if 0 <= r < H:
        wet = mask_ref[r : r + 1, :].astype(F32)
        return init_ref[:, r, :] * wet, wet, target_ref[:, r, :]
    ref, k = (below_ref, r + REACH) if r < 0 else (above_ref, r - H)
    field = ref[k * 8 : k * 8 + 8, :]
    m = r + H if r < 0 else r - H
    wet = ref[64 + m : 65 + m, :]
    target = None
    if -2 <= r < H + 2:
        t = r + 2 if r < 0 else r - H
        target = ref[48 + 8 * t : 56 + 8 * t, :]
    return field, wet, target


def pack_cols(init_ref, target_ref, mask_ref, below_ref, above_ref, left_ref, right_ref):
    lane = lax.broadcasted_iota(jnp.int32, (8, 128), 1)
    for r in range(-REACH, H + REACH):
        field, wet, target = row_parts(r, init_ref, target_ref, mask_ref, below_ref, above_ref)
        wet = jnp.broadcast_to(wet, (8, W))
        a = jnp.where(lane < 32, field[:, :128], turned(wet[:, :128], 32))
        b = jnp.where(lane >= 96, field[:, 128:], turned(wet[:, 128:], -32))
        if target is not None:
            a = jnp.where(lane < 64, a, turned(target[:, :128], 64))
            b = jnp.where(lane >= 64, b, turned(target[:, 128:], -64))
        at = (r + REACH) * 8
        left_ref[at : at + 8, :] = a
        right_ref[at : at + 8, :] = b


def prepare(one_ref, two_ref, head_ref, w1_ref, w2_ref, w3_ref, w3t_ref, w2t_ref, w1t_ref, bias_ref):
    one, two, head = one_ref[...], two_ref[...], head_ref[...]
    w1_ref[...] = one[:, : 9 * LEV].astype(BF)
    w2_ref[...] = two[:, : 9 * C].astype(BF)
    w3_ref[...] = head[:, :C].astype(BF)
    w3t_ref[...] = head[:, :C].T.astype(BF)
    w2t_ref[...] = jnp.concatenate(
        [two[:, (8 - k) * C : (9 - k) * C].T for k in range(9)], axis=1
    ).astype(BF)
    w1t_ref[...] = jnp.concatenate(
        [
            jnp.concatenate(
                [one[:, (3 * (2 - a) + b) * LEV : (3 * (2 - a) + b + 1) * LEV].T for a in range(3)],
                axis=1,
            )
            for b in range(3)
        ],
        axis=0,
    ).astype(BF)
    bias_ref[0:64, :] = jnp.broadcast_to(one[:, 9 * LEV :], (64, 128))
    bias_ref[64:128, :] = jnp.broadcast_to(two[:, 9 * C :], (64, 128))
    bias_ref[128:160, :] = jnp.broadcast_to(head[:, C:], (32, 128))


def lanes(parts):
    return parts[0] if len(parts) == 1 else jnp.concatenate(parts, axis=1)


def cut(v, n):
    return [v[:, k * PITCH : (k + 1) * PITCH] for k in range(n)]


def folded(v):
    total = v[:, :128]
    for k in range(1, v.shape[1] // 128):
        total = total + v[:, k * 128 : (k + 1) * 128]
    return total


def main(
    init_ref, target_ref, mask_ref, below_ref, above_ref, fromleft_ref, fromright_ref,
    w1_ref, w2_ref, w3_ref, w3t_ref, w2t_ref, w1t_ref, bias_ref,
    final_ref, grad_ref,
    xc0, xc1, wet_s, tgt, hc0, hc1, h2s, sp10, sp11, sp2, wd, ec0, ec1, e1s, rem, up, down, fin,
    b1g, b2g, b3g, g1, g2, g3,
):
    lane = lax.broadcasted_iota(jnp.int32, (8, 128), 1)
    zero = jnp.zeros((8, 128), F32)
    for r in range(-REACH, H + REACH):
        field, wet, target = row_parts(r, init_ref, target_ref, mask_ref, below_ref, above_ref)
        at = (r + REACH) * 8
        fl, fr = fromleft_ref[at : at + 8, :], fromright_ref[at : at + 8, :]

        def rim(by):
            right, left = (turned(fr, -by), turned(fl, by)) if by else (fr, fl)
            return jnp.where(lane < 16, right, jnp.where(lane >= 112, left, zero))

        row = jnp.concatenate([field, rim(0)], axis=1)
        xc0[at * 3 : at * 3 + 24, :] = jnp.concatenate(
            [turned(row, 1), row, turned(row, -1)], axis=0
        )
        wet_s[at : at + 8, :] = jnp.concatenate([jnp.broadcast_to(wet, (8, W)), rim(32)], axis=1)
        if target is not None:
            tgt[at : at + 8, :] = jnp.concatenate([target, rim(64)], axis=1)
    for ref in (b1g, b2g, b3g, g1, g2, g3):
        ref[...] = jnp.zeros(ref.shape, F32)
    for r in (4, 5, 14, 15):
        ec0[r * 192 : r * 192 + 192, :] = jnp.zeros((192, PITCH), BF)

    col = lax.broadcasted_iota(jnp.int32, (1, PITCH), 1)
    col = jnp.where(col < 320, col, col - PITCH) + lax.axis_index(GY) * W
    col_in = jnp.where((col >= 0) & (col < lax.axis_size(GY) * W), 1.0, 0.0).astype(F32)

    row0 = lax.axis_index("gx") * H

    def inside(r):
        i = row0 + r - REACH
        return col_in * jnp.where((i >= 0) & (i < lax.axis_size("gx") * H), 1.0, 0.0)

    def bias(at, n, times=1):
        b = bias_ref[at : at + n, :]
        return jnp.concatenate([b] * (3 * times), axis=1)

    def part(ref, r, size, first=0, count=None):
        start = r * size + first
        return ref.at[start : start + (size if count is None else count), :]

    def loop(lo, hi, per, body):
        for first in range(lo, hi, per):
            body([first + REACH + k for k in range(per)])

    def thrice(v):
        return turned(v, 1), v, turned(v, -1)

    def store_thrice(ref, r, v):
        for k, piece in enumerate(thrice(v)):
            part(ref, r, 192, 64 * k, 64)[...] = piece.astype(BF)

    def first_layer(xc, hc, sp1):
        def body(rs):
            x9 = lanes([part(xc, r - 1, 24, 0, 72)[...].astype(BF) for r in rs])
            for r, z in zip(rs, cut(dot(w1_ref[...], x9), len(rs))):
                z = z + bias(0, 64)
                s = sigmoid(z)
                keep = inside(r)
                store_thrice(hc, r, z * s * keep)
                part(sp1, r, 64)[...] = silu_slope(z, s) * keep

        return body

    def second_layer(hc, rs):
        z = dot(w2_ref[...], lanes([part(hc, r - 1, 192, 0, 576)[...] for r in rs]))
        z = z + bias(64, 64, len(rs))
        s = sigmoid(z)
        h2 = (z * s).astype(BF)
        q = dot(w3_ref[...], h2) + bias(128, 32, len(rs))
        return h2, silu_slope(z, s), sigmoid(q)

    def slopes(xc, r):
        x = part(xc, r, 24, 8, 8)[...]
        beside = (
            part(xc, r + 1, 24, 8, 8)[...],
            part(xc, r - 1, 24, 8, 8)[...],
            part(xc, r, 24, 16, 8)[...],
            part(xc, r, 24, 0, 8)[...],
        )
        return x, [b - x for b in beside]

    def tail_zero(rs):
        h2, slope, p = second_layer(hc0, rs)
        n = len(rs)
        for r, h2r, sr, pr in zip(rs, cut(h2, n), cut(slope, n), cut(p, n)):
            part(h2s, r, 64)[...] = h2r
            part(sp2, r, 64)[...] = sr
            x, diff = slopes(xc0, r)
            wet = part(wet_s, r, 8)[...]
            change = jnp.zeros_like(x)
            for k in range(4):
                pk = pr[8 * k : 8 * k + 8]
                move = 0.25 * pk * diff[k]
                change = change + move
                part(wd, r, 32, 8 * k, 8)[...] = wet * move * (1.0 - pk)
            for k, piece in enumerate(thrice(x + wet * change)):
                part(xc1, r, 24, 8 * k, 8)[...] = piece

    def tail_grads(rs, e3, e2, h2, hc):
        b3g[...] += sum(folded(e[:, :W]) for e in e3)
        b2g[...] += sum(folded(e[:, :W]) for e in e2)
        g3[...] += dot_nt(
            lanes([e[:, :W].astype(BF) for e in e3]), lanes([v[:, :W] for v in h2])
        )
        g2[...] += dot_nt(
            lanes([e[:, :W].astype(BF) for e in e2]),
            lanes([part(hc, r - 1, 192, 0, 576)[:, :W] for r in rs]),
        )

    def tail_one(own):
        def body(rs):
            h2, slope, p = second_layer(hc1, rs)
            n = len(rs)
            e3s = []
            for r, pr in zip(rs, cut(p, n)):
                x, diff = slopes(xc1, r)
                wet = part(wet_s, r, 8)[...]
                c = [0.25 * pr[8 * k : 8 * k + 8] for k in range(4)]
                move = [c[k] * diff[k] for k in range(4)]
                new = x + wet * (move[0] + move[1] + move[2] + move[3])
                if own:
                    part(fin, r, 8)[...] = new
                g = wet * (new - part(tgt, r, 8)[...])
                wg = wet * g
                t = [wg * c[k] for k in range(4)]
                left = g - t[0] - t[1] - t[2] - t[3]
                part(rem, r, 8)[...] = left + turned(t[2], 1) + turned(t[3], -1)
                part(up, r, 8)[...] = t[0]
                part(down, r, 8)[...] = t[1]
                e3s.append(
                    jnp.concatenate(
                        [wg * move[k] * (1.0 - pr[8 * k : 8 * k + 8]) for k in range(4)], axis=0
                    )
                )
            e2 = dot(w3t_ref[...], lanes([e.astype(BF) for e in e3s])) * slope
            e2s = cut(e2, n)
            for r, e in zip(rs, e2s):
                store_thrice(ec1, r, e)
            if own:
                tail_grads(rs, e3s, e2s, cut(h2, n), hc1)

        return body

    def first_error(ec, sp1, rs):
        e = dot(w2t_ref[...], lanes([part(ec, r - 1, 192, 0, 576)[...] for r in rs]))
        return [v * part(sp1, r, 64)[...] for r, v in zip(rs, cut(e, len(rs)))]

    def first_grads(rs, e1, xc, width):
        b1g[...] += sum(folded(e[:, :width]) for e in e1)
        g1[...] += dot_nt(
            lanes([e[:, :width].astype(BF) for e in e1]),
            lanes([part(xc, r - 1, 24, 0, 72)[:, :width].astype(BF) for r in rs]),
        )

    def first_one(own):
        def body(rs):
            e1 = first_error(ec1, sp11, rs)
            for r, e in zip(rs, e1):
                part(e1s, r, 64)[...] = e.astype(BF)
            if own:
                first_grads(rs, e1, xc1, W)

        return body

    def back_zero(rs):
        y = dot(w1t_ref[...], lanes([part(e1s, r - 1, 64, 0, 192)[...] for r in rs]))
        e3s = []
        for r, yr in zip(rs, cut(y, len(rs))):
            g = part(rem, r, 8)[...] + part(up, r - 1, 8)[...] + part(down, r + 1, 8)[...]
            g = g + yr[8:16] + turned(yr[0:8], -1) + turned(yr[16:24], 1)
            e3 = jnp.concatenate([g] * 4, axis=0) * part(wd, r, 32)[...]
            e3s.append(jnp.concatenate([e3[:, :W], jnp.zeros((K, PITCH - W), F32)], axis=1))
        e2 = dot(w3t_ref[...], lanes([e.astype(BF) for e in e3s]))
        e2s = [v * part(sp2, r, 64)[...] for r, v in zip(rs, cut(e2, len(rs)))]
        for r, e in zip(rs, e2s):
            store_thrice(ec0, r, e)
        tail_grads(rs, e3s, e2s, [part(h2s, r, 64)[...] for r in rs], hc0)

    def first_zero(rs):
        first_grads(rs, first_error(ec0, sp10, rs), xc0, PITCH)

    loop(-5, 13, 9, first_layer(xc0, hc0, sp10))
    loop(-4, 12, 16, tail_zero)
    loop(-3, 11, 14, first_layer(xc1, hc1, sp11))
    tail_one(False)([4, 5, 14, 15])
    loop(0, 8, 8, tail_one(True))
    first_one(False)([5, 14])
    loop(0, 8, 8, first_one(True))
    loop(0, 8, 8, back_zero)
    loop(-1, 9, 10, first_zero)

    for r in range(H):
        final_ref[:, r, :] = fin[(r + REACH) * 8 : (r + REACH) * 8 + 8, :W]
    for k in range(4):
        grad_ref[k * 64 : k * 64 + 64, :] = g2[:, k * 128 : k * 128 + 128]
    grad_ref[256:320, :] = jnp.concatenate([g2[:, 512:576], g1[:, 0:64]], axis=1)
    sums = [jnp.sum(ref[...], axis=1, keepdims=True) for ref in (b1g, b2g, b3g)]
    sums[2] = jnp.concatenate([sums[2], jnp.zeros((32, 1), F32)], axis=0)
    grad_ref[320:384, :] = jnp.concatenate(
        [
            g1[:, 64:72],
            *sums,
            jnp.zeros((64, 53), F32),
            jnp.concatenate([g3[...], jnp.zeros((32, 64), F32)], axis=0),
        ],
        axis=1,
    )


def row_sums(parts):
    return jnp.concatenate([jnp.sum(v * v, axis=1, keepdims=True) for v in parts], axis=0)


def groups(d1_ref, d2_ref, d3_ref, gid_ref, choose_ref, below_ref):
    group = lax.broadcasted_iota(jnp.int32, (128, 160), 0)
    choose = jnp.where(gid_ref[...] == group, 1.0, 0.0).T
    choose_ref[...] = choose
    sums = jnp.sum(choose * row_sums((d1_ref[...], d2_ref[...], d3_ref[...])), axis=0, keepdims=True)
    below_ref[...] = jnp.sqrt(sums + 1e-06)


def finish(total_ref, d1_ref, d2_ref, d3_ref, choose_ref, below_ref, u1_ref, u2_ref, u3_ref):
    t = [total_ref[k * 64 : k * 64 + 64, :] for k in range(6)]
    two = jnp.concatenate([*t[:4], t[4][:, :64], t[5][:, 9:10]], axis=1)
    one = jnp.concatenate([t[4][:, 64:], t[5][:, :8], t[5][:, 8:9]], axis=1)
    three = jnp.concatenate([t[5][:32, 64:], t[5][:32, 10:11]], axis=1)
    grads = (one, two, three)
    norm = jnp.sqrt(jnp.sum(row_sums(grads), axis=0, keepdims=True))
    factor = 1.0 / jnp.maximum(norm, 1.0)
    clipped = [v * factor for v in grads]
    choose = choose_ref[...]
    ratios = jnp.sqrt(jnp.sum(choose * row_sums(clipped), axis=0, keepdims=True)) / below_ref[...]
    row_ratio = jnp.sum(choose * ratios, axis=1, keepdims=True)
    scaling = math.sqrt(PARAMS)
    at = 0
    for ref, v, d_ref in zip((u1_ref, u2_ref, u3_ref), clipped, (d1_ref, d2_ref, d3_ref)):
        n = v.shape[0]
        ref[...] = scaling * (v + row_ratio[at : at + n] * d_ref[...])
        at += n


def shape(dims, dtype=F32):
    return jax.ShapeDtypeStruct(dims, dtype)


def kernel(body, outs, cost, mib, **more):
    return pl.pallas_call(
        body,
        out_shape=outs,
        cost_estimate=pl.CostEstimate(flops=cost, bytes_accessed=cost, transcendentals=0),
        compiler_params=pltpu.CompilerParams(vmem_limit_bytes=mib * 2**20),
        **more,
    )


def exchange(forward, backward, axis):
    count = lax.axis_size(axis)
    ahead = [(i, i + 1) for i in range(count - 1)]
    back = [(b, a) for a, b in ahead]
    return lax.ppermute(forward, axis, ahead), lax.ppermute(backward, axis, back)


def total_of(grad):
    near, far = ("gy_0", "gy_1"), ("gx", "gy_2")
    n = lax.axis_size(near)
    pieces = grad.reshape(n, -1, 128)
    own = jnp.sum(lax.all_to_all(pieces, near, 0, 0, tiled=True), axis=0)
    m = lax.axis_size(far)
    copies = jnp.broadcast_to(own, (m, *own.shape))
    own = jnp.sum(lax.all_to_all(copies, far, 0, 0, tiled=True), axis=0)
    copies = jnp.broadcast_to(own, (n, *own.shape))
    return lax.all_to_all(copies, near, 0, 0, tiled=True).reshape(grad.shape)


def per_device(init, target, mask, one, two, head, d1, d2, d3, gid):
    to_low, to_high = kernel(pack_rows, [shape((72, W))] * 2, 10**5, 4)(init, target, mask)
    below, above = exchange(to_high, to_low, "gx")
    weights = kernel(
        prepare,
        [
            shape((C, 72), BF), shape((C, 576), BF), shape((K, C), BF), shape((C, K), BF),
            shape((C, 576), BF), shape((24, 192), BF), shape((160, 128)),
        ],
        10**6,
        8,
    )(one, two, head)
    choose, below_ratio = kernel(groups, [shape((160, 128)), shape((1, 128))], 10**6, 8)(
        d1, d2, d3, gid.reshape(1, -1)
    )
    to_left, to_right = kernel(pack_cols, [shape((160, 128))] * 2, 10**5, 4)(
        init, target, mask, below, above
    )
    from_left, from_right = exchange(to_right, to_left, GY)

    def rows(size, dtype=F32):
        return pltpu.VMEM((20 * size, PITCH), dtype)

    final, grad = kernel(
        main,
        [shape((LEV, H, W)), shape((384, 128))],
        10**7,
        40,
        scratch_shapes=[
            rows(24), rows(24), rows(8), rows(8), rows(192, BF), rows(192, BF), rows(64, BF),
            rows(64), rows(64), rows(64), rows(32), rows(192, BF), rows(192, BF), rows(64, BF),
            rows(8), rows(8), rows(8), rows(8),
            pltpu.VMEM((64, 128), F32), pltpu.VMEM((64, 128), F32), pltpu.VMEM((32, 128), F32),
            pltpu.VMEM((64, 72), F32), pltpu.VMEM((64, 576), F32), pltpu.VMEM((32, 64), F32),
        ],
    )(init, target, mask, below, above, from_left, from_right, *weights)
    total = total_of(grad)
    u1, u2, u3 = kernel(finish, [shape(one.shape), shape(two.shape), shape(head.shape)], 10**6, 8)(
        total, d1, d2, d3, choose, below_ratio
    )
    return final, u1, u2, u3


def solution(mesh):
    count = mesh.shape["gy"] // 8
    torus = Mesh(mesh.devices.reshape(mesh.shape["gx"], count, 4, 2), ("gx", *GY))
    placed = (P(None, "gx", GY), P(None, "gx", GY), P("gx", GY), P(), P(), P(), P(), P(), P(), P())
    return jax.shard_map(
        per_device,
        mesh=torus,
        in_specs=placed,
        out_specs=(P(None, "gx", GY), P(), P(), P()),
        check_vma=False,
    )
```

```python
import math

import jax
import jax.numpy as jnp
from jax import lax
from jax.experimental import pallas as pl
from jax.experimental.pallas import tpu as pltpu
from jax.sharding import Mesh
from jax.sharding import PartitionSpec as P

LEV = 8
C = 64
K = 32
GROUPS = 6
PARAMS = 43680
GY = ("gy_0", "gy_1", "gy_2")
H = 8
W = 256
PITCH = 384
REACH = 6
BF = jnp.bfloat16
F32 = jnp.float32
NT = (((1,), (1,)), ((), ()))


def dot(a, b):
    return jnp.dot(a, b, preferred_element_type=F32)


def dot_nt(a, b):
    return lax.dot_general(a, b, NT, preferred_element_type=F32)


def turned(v, by):
    return pltpu.roll(v, by % v.shape[1], 1)


def sigmoid(v):
    return 0.5 * jnp.tanh(0.5 * v) + 0.5


def silu_slope(v, s):
    return s * (1.0 + v * (1.0 - s))


def pack_rows(init_ref, target_ref, mask_ref, low_ref, high_ref):
    wet = mask_ref[...].astype(F32)
    low_ref[64:72, :] = wet
    high_ref[64:72, :] = wet
    for k in range(REACH):
        low_ref[k * 8 : k * 8 + 8, :] = init_ref[:, k, :] * wet[k : k + 1]
        r = H - REACH + k
        high_ref[k * 8 : k * 8 + 8, :] = init_ref[:, r, :] * wet[r : r + 1]
    for k in range(2):
        low_ref[48 + k * 8 : 56 + k * 8, :] = target_ref[:, k, :]
        high_ref[48 + k * 8 : 56 + k * 8, :] = target_ref[:, H - 2 + k, :]


def row_parts(r, init_ref, target_ref, mask_ref, below_ref, above_ref):
    if 0 <= r < H:
        wet = mask_ref[r : r + 1, :].astype(F32)
        return init_ref[:, r, :] * wet, wet, target_ref[:, r, :]
    ref, k = (below_ref, r + REACH) if r < 0 else (above_ref, r - H)
    field = ref[k * 8 : k * 8 + 8, :]
    m = r + H if r < 0 else r - H
    wet = ref[64 + m : 65 + m, :]
    target = None
    if -2 <= r < H + 2:
        t = r + 2 if r < 0 else r - H
        target = ref[48 + 8 * t : 56 + 8 * t, :]
    return field, wet, target


def pack_cols(init_ref, target_ref, mask_ref, below_ref, above_ref, left_ref, right_ref):
    lane = lax.broadcasted_iota(jnp.int32, (8, 128), 1)
    zero = jnp.zeros((8, 128), F32)
    packed = [zero] * 6
    for r in range(-REACH, H + REACH):
        field, wet, target = row_parts(r, init_ref, target_ref, mask_ref, below_ref, above_ref)
        wet = jnp.broadcast_to(wet, (8, W))
        at, by = divmod(r + REACH, 8)
        inner = lane - 16 * by
        for side, first, moves in ((0, 0, (0, 6, 10)), (3, 128, (6, 10, 12))):
            move = [by * 16 + m for m in moves]
            v = turned(field[:, first : first + 128], move[0])
            v = jnp.where(inner < 6, v, turned(wet[:, first : first + 128], move[1]))
            if target is not None:
                v = jnp.where(inner < 10, v, turned(target[:, first : first + 128], move[2]))
            packed[side + at] = jnp.where((inner >= 0) & (inner < 12), v, packed[side + at])
    for k in range(3):
        left_ref[k * 8 : k * 8 + 8, :] = packed[k]
        right_ref[k * 8 : k * 8 + 8, :] = packed[3 + k]


def row_sums(parts):
    return jnp.concatenate([jnp.sum(v * v, axis=1, keepdims=True) for v in parts], axis=0)


def prepare(
    one_ref, two_ref, head_ref, d1_ref, d2_ref, d3_ref, gid_ref,
    w1_ref, w2_ref, w3_ref, w3t_ref, w2t_ref, w1t_ref, bias_ref, choose_ref, below_ref,
):
    one, two, head = one_ref[...], two_ref[...], head_ref[...]
    w1_ref[...] = one[:, : 9 * LEV].astype(BF)
    w2_ref[...] = two[:, : 9 * C].astype(BF)
    w3_ref[...] = head[:, :C].astype(BF)
    w3t_ref[...] = head[:, :C].T.astype(BF)
    w2t_ref[...] = jnp.concatenate(
        [two[:, (8 - k) * C : (9 - k) * C].T for k in range(9)], axis=1
    ).astype(BF)
    w1t_ref[...] = jnp.concatenate(
        [
            jnp.concatenate(
                [one[:, (3 * (2 - a) + b) * LEV : (3 * (2 - a) + b + 1) * LEV].T for a in range(3)],
                axis=1,
            )
            for b in range(3)
        ],
        axis=0,
    ).astype(BF)
    bias_ref[0:64, :] = jnp.broadcast_to(one[:, 9 * LEV :], (64, 128))
    bias_ref[64:128, :] = jnp.broadcast_to(two[:, 9 * C :], (64, 128))
    bias_ref[128:160, :] = jnp.broadcast_to(head[:, C:], (32, 128))
    group = lax.broadcasted_iota(jnp.int32, (128, 160), 0)
    choose = jnp.where(gid_ref[...] == group, 1.0, 0.0).T
    choose_ref[...] = choose
    sums = jnp.sum(choose * row_sums((d1_ref[...], d2_ref[...], d3_ref[...])), axis=0, keepdims=True)
    below_ref[...] = jnp.sqrt(sums + 1e-06)


def lanes(parts):
    return parts[0] if len(parts) == 1 else jnp.concatenate(parts, axis=1)


def cut(v, n):
    return [v[:, k * PITCH : (k + 1) * PITCH] for k in range(n)]


def folded(v):
    total = v[:, :128]
    for k in range(1, v.shape[1] // 128):
        total = total + v[:, k * 128 : (k + 1) * 128]
    return total


def main(
    init_ref, target_ref, mask_ref, below_ref, above_ref, fromleft_ref, fromright_ref,
    w1_ref, w2_ref, w3_ref, w3t_ref, w2t_ref, w1t_ref, bias_ref,
    final_ref, grad_ref,
    xc0, xc1, wet_s, tgt, hc0, hc1, h2s, sp10, sp11, sp2, wd, ec0, ec1, e1s, rem, up, down, fin,
    b1g, b2g, b3g, g1, g2, g3, final_v, sem,
):
    lane = lax.broadcasted_iota(jnp.int32, (8, 128), 1)
    zero = jnp.zeros((8, 128), F32)
    for r in range(-REACH, H + REACH):
        field, wet, target = row_parts(r, init_ref, target_ref, mask_ref, below_ref, above_ref)
        at = (r + REACH) * 8
        block, by = divmod(r + REACH, 8)
        fl = fromleft_ref[block * 8 : block * 8 + 8, :]
        fr = fromright_ref[block * 8 : block * 8 + 8, :]

        def rim(first, width):
            right = turned(fr, -(by * 16 + first))
            left = turned(fl, -(by * 16 + first) - width)
            return jnp.where(lane < width, right, jnp.where(lane >= 128 - width, left, zero))

        row = jnp.concatenate([field, rim(0, 6)], axis=1)
        xc0[at * 3 : at * 3 + 24, :] = jnp.concatenate(
            [turned(row, 1), row, turned(row, -1)], axis=0
        )
        wet_s[at : at + 8, :] = jnp.concatenate([jnp.broadcast_to(wet, (8, W)), rim(6, 4)], axis=1)
        if target is not None:
            tgt[at : at + 8, :] = jnp.concatenate([target, rim(10, 2)], axis=1)
    for ref in (b1g, b2g, b3g, g1, g2, g3):
        ref[...] = jnp.zeros(ref.shape, F32)
    for r in (4, 5, 14, 15):
        ec0[r * 192 : r * 192 + 192, :] = jnp.zeros((192, PITCH), BF)

    col = lax.broadcasted_iota(jnp.int32, (1, PITCH), 1)
    col = jnp.where(col < 320, col, col - PITCH) + lax.axis_index(GY) * W
    col_in = jnp.where((col >= 0) & (col < lax.axis_size(GY) * W), 1.0, 0.0).astype(F32)

    row0 = lax.axis_index("gx") * H

    def inside(r):
        i = row0 + r - REACH
        return col_in * jnp.where((i >= 0) & (i < lax.axis_size("gx") * H), 1.0, 0.0)

    def bias(at, n, times=1):
        b = bias_ref[at : at + n, :]
        return jnp.concatenate([b] * (3 * times), axis=1)

    def part(ref, r, size, first=0, count=None):
        start = r * size + first
        return ref.at[start : start + (size if count is None else count), :]

    def loop(lo, hi, per, body):
        for first in range(lo, hi, per):
            body([first + REACH + k for k in range(per)])

    def thrice(v):
        return turned(v, 1), v, turned(v, -1)

    def store_thrice(ref, r, v):
        for k, piece in enumerate(thrice(v)):
            part(ref, r, 192, 64 * k, 64)[...] = piece.astype(BF)

    def first_layer(xc, hc, sp1):
        def body(rs):
            x9 = lanes([part(xc, r - 1, 24, 0, 72)[...].astype(BF) for r in rs])
            for r, z in zip(rs, cut(dot(w1_ref[...], x9), len(rs))):
                z = z + bias(0, 64)
                s = sigmoid(z)
                keep = inside(r)
                store_thrice(hc, r, z * s * keep)
                part(sp1, r, 64)[...] = silu_slope(z, s) * keep

        return body

    def second_layer(hc, rs):
        z = dot(w2_ref[...], lanes([part(hc, r - 1, 192, 0, 576)[...] for r in rs]))
        z = z + bias(64, 64, len(rs))
        s = sigmoid(z)
        h2 = (z * s).astype(BF)
        q = dot(w3_ref[...], h2) + bias(128, 32, len(rs))
        return h2, silu_slope(z, s), sigmoid(q)

    def slopes(xc, r):
        x = part(xc, r, 24, 8, 8)[...]
        beside = (
            part(xc, r + 1, 24, 8, 8)[...],
            part(xc, r - 1, 24, 8, 8)[...],
            part(xc, r, 24, 16, 8)[...],
            part(xc, r, 24, 0, 8)[...],
        )
        return x, [b - x for b in beside]

    def tail_zero(rs):
        h2, slope, p = second_layer(hc0, rs)
        n = len(rs)
        for r, h2r, sr, pr in zip(rs, cut(h2, n), cut(slope, n), cut(p, n)):
            part(h2s, r, 64)[...] = h2r
            part(sp2, r, 64)[...] = sr
            x, diff = slopes(xc0, r)
            wet = part(wet_s, r, 8)[...]
            change = jnp.zeros_like(x)
            for k in range(4):
                pk = pr[8 * k : 8 * k + 8]
                move = 0.25 * pk * diff[k]
                change = change + move
                part(wd, r, 32, 8 * k, 8)[...] = wet * move * (1.0 - pk)
            for k, piece in enumerate(thrice(x + wet * change)):
                part(xc1, r, 24, 8 * k, 8)[...] = piece

    def tail_grads(rs, e3, e2, h2, hc):
        b3g[...] += sum(folded(e[:, :W]) for e in e3)
        b2g[...] += sum(folded(e[:, :W]) for e in e2)
        g3[...] += dot_nt(
            lanes([e[:, :W].astype(BF) for e in e3]), lanes([v[:, :W] for v in h2])
        )
        g2[...] += dot_nt(
            lanes([e[:, :W].astype(BF) for e in e2]),
            lanes([part(hc, r - 1, 192, 0, 576)[:, :W] for r in rs]),
        )

    def tail_one(own):
        def body(rs):
            h2, slope, p = second_layer(hc1, rs)
            n = len(rs)
            e3s = []
            for r, pr in zip(rs, cut(p, n)):
                x, diff = slopes(xc1, r)
                wet = part(wet_s, r, 8)[...]
                c = [0.25 * pr[8 * k : 8 * k + 8] for k in range(4)]
                move = [c[k] * diff[k] for k in range(4)]
                new = x + wet * (move[0] + move[1] + move[2] + move[3])
                if own:
                    part(fin, r, 8)[...] = new
                g = wet * (new - part(tgt, r, 8)[...])
                wg = wet * g
                t = [wg * c[k] for k in range(4)]
                left = g - t[0] - t[1] - t[2] - t[3]
                part(rem, r, 8)[...] = left + turned(t[2], 1) + turned(t[3], -1)
                part(up, r, 8)[...] = t[0]
                part(down, r, 8)[...] = t[1]
                e3s.append(
                    jnp.concatenate(
                        [wg * move[k] * (1.0 - pr[8 * k : 8 * k + 8]) for k in range(4)], axis=0
                    )
                )
            e2 = dot(w3t_ref[...], lanes([e.astype(BF) for e in e3s])) * slope
            e2s = cut(e2, n)
            for r, e in zip(rs, e2s):
                store_thrice(ec1, r, e)
            if own:
                tail_grads(rs, e3s, e2s, cut(h2, n), hc1)

        return body

    def first_error(ec, sp1, rs):
        e = dot(w2t_ref[...], lanes([part(ec, r - 1, 192, 0, 576)[...] for r in rs]))
        return [v * part(sp1, r, 64)[...] for r, v in zip(rs, cut(e, len(rs)))]

    def first_grads(rs, e1, xc, width):
        b1g[...] += sum(folded(e[:, :width]) for e in e1)
        g1[...] += dot_nt(
            lanes([e[:, :width].astype(BF) for e in e1]),
            lanes([part(xc, r - 1, 24, 0, 72)[:, :width].astype(BF) for r in rs]),
        )

    def first_one(own):
        def body(rs):
            e1 = first_error(ec1, sp11, rs)
            for r, e in zip(rs, e1):
                part(e1s, r, 64)[...] = e.astype(BF)
            if own:
                first_grads(rs, e1, xc1, W)

        return body

    def back_zero(rs):
        y = dot(w1t_ref[...], lanes([part(e1s, r - 1, 64, 0, 192)[...] for r in rs]))
        e3s = []
        for r, yr in zip(rs, cut(y, len(rs))):
            g = part(rem, r, 8)[...] + part(up, r - 1, 8)[...] + part(down, r + 1, 8)[...]
            g = g + yr[8:16] + turned(yr[0:8], -1) + turned(yr[16:24], 1)
            e3 = jnp.concatenate([g] * 4, axis=0) * part(wd, r, 32)[...]
            e3s.append(jnp.concatenate([e3[:, :W], jnp.zeros((K, PITCH - W), F32)], axis=1))
        e2 = dot(w3t_ref[...], lanes([e.astype(BF) for e in e3s]))
        e2s = [v * part(sp2, r, 64)[...] for r, v in zip(rs, cut(e2, len(rs)))]
        for r, e in zip(rs, e2s):
            store_thrice(ec0, r, e)
        tail_grads(rs, e3s, e2s, [part(h2s, r, 64)[...] for r in rs], hc0)

    def first_zero(rs):
        first_grads(rs, first_error(ec0, sp10, rs), xc0, PITCH)

    loop(-5, 13, 9, first_layer(xc0, hc0, sp10))
    loop(-4, 12, 16, tail_zero)
    loop(-3, 11, 14, first_layer(xc1, hc1, sp11))
    tail_one(False)([4, 5, 14, 15])
    loop(0, 8, 8, tail_one(True))
    for r in range(H):
        final_v[:, r, :] = fin[(r + REACH) * 8 : (r + REACH) * 8 + 8, :W]
    out = pltpu.make_async_copy(final_v, final_ref, sem)
    out.start()
    first_one(False)([5, 14])
    loop(0, 8, 8, first_one(True))
    loop(0, 8, 8, back_zero)
    loop(-1, 9, 10, first_zero)

    for k in range(4):
        grad_ref[k * 64 : k * 64 + 64, :] = g2[:, k * 128 : k * 128 + 128]
    grad_ref[256:320, :] = jnp.concatenate([g2[:, 512:576], g1[:, 0:64]], axis=1)
    sums = [jnp.sum(ref[...], axis=1, keepdims=True) for ref in (b1g, b2g, b3g)]
    sums[2] = jnp.concatenate([sums[2], jnp.zeros((32, 1), F32)], axis=0)
    grad_ref[320:384, :] = jnp.concatenate(
        [
            g1[:, 64:72],
            *sums,
            jnp.zeros((64, 53), F32),
            jnp.concatenate([g3[...], jnp.zeros((32, 64), F32)], axis=0),
        ],
        axis=1,
    )
    out.wait()


def finish(total_ref, d1_ref, d2_ref, d3_ref, choose_ref, below_ref, u1_ref, u2_ref, u3_ref):
    t = [total_ref[k * 64 : k * 64 + 64, :] for k in range(6)]
    two = jnp.concatenate([*t[:4], t[4][:, :64], t[5][:, 9:10]], axis=1)
    one = jnp.concatenate([t[4][:, 64:], t[5][:, :8], t[5][:, 8:9]], axis=1)
    three = jnp.concatenate([t[5][:32, 64:], t[5][:32, 10:11]], axis=1)
    grads = (one, two, three)
    norm = jnp.sqrt(jnp.sum(row_sums(grads), axis=0, keepdims=True))
    factor = 1.0 / jnp.maximum(norm, 1.0)
    clipped = [v * factor for v in grads]
    choose = choose_ref[...]
    ratios = jnp.sqrt(jnp.sum(choose * row_sums(clipped), axis=0, keepdims=True)) / below_ref[...]
    row_ratio = jnp.sum(choose * ratios, axis=1, keepdims=True)
    scaling = math.sqrt(PARAMS)
    at = 0
    for ref, v, d_ref in zip((u1_ref, u2_ref, u3_ref), clipped, (d1_ref, d2_ref, d3_ref)):
        n = v.shape[0]
        ref[...] = scaling * (v + row_ratio[at : at + n] * d_ref[...])
        at += n


def shape(dims, dtype=F32):
    return jax.ShapeDtypeStruct(dims, dtype)


def kernel(body, outs, cost, mib, **more):
    return pl.pallas_call(
        body,
        out_shape=outs,
        cost_estimate=pl.CostEstimate(flops=cost, bytes_accessed=cost, transcendentals=0),
        compiler_params=pltpu.CompilerParams(vmem_limit_bytes=mib * 2**20),
        **more,
    )


def exchange(forward, backward, axis):
    count = lax.axis_size(axis)
    ahead = [(i, i + 1) for i in range(count - 1)]
    back = [(b, a) for a, b in ahead]
    return lax.ppermute(forward, axis, ahead), lax.ppermute(backward, axis, back)


def total_of(grad):
    near = ("gy_0", "gy_1")
    n = lax.axis_size(near)
    pieces = grad.reshape(n, -1, 128)
    own = jnp.sum(lax.all_to_all(pieces, near, 0, 0, tiled=True), axis=0)
    own = own + lax.ppermute(own, "gy_2", [(0, 1), (1, 0)])
    m = lax.axis_size("gx")
    copies = jnp.broadcast_to(own, (m, *own.shape))
    own = jnp.sum(lax.all_to_all(copies, "gx", 0, 0, tiled=True), axis=0)
    copies = jnp.broadcast_to(own, (n, *own.shape))
    return lax.all_to_all(copies, near, 0, 0, tiled=True).reshape(grad.shape)


def per_device(init, target, mask, one, two, head, d1, d2, d3, gid):
    hbm = pl.BlockSpec(memory_space=pltpu.HBM)
    vmem = pl.BlockSpec(memory_space=pltpu.VMEM)
    to_low, to_high = kernel(pack_rows, [shape((72, W))] * 2, 10**5, 60)(init, target, mask)
    below, above = exchange(to_high, to_low, "gx")
    to_left, to_right = kernel(pack_cols, [shape((24, 128))] * 2, 10**5, 4)(
        init, target, mask, below, above
    )
    from_left, from_right = exchange(to_right, to_left, GY)
    *weights, choose, below_ratio = kernel(
        prepare,
        [
            shape((C, 72), BF), shape((C, 576), BF), shape((K, C), BF), shape((C, K), BF),
            shape((C, 576), BF), shape((24, 192), BF), shape((160, 128)),
            shape((160, 128)), shape((1, 128)),
        ],
        10**6,
        8,
    )(one, two, head, d1, d2, d3, gid.reshape(1, -1))

    def rows(size, dtype=F32):
        return pltpu.VMEM((20 * size, PITCH), dtype)

    final, grad = kernel(
        main,
        [shape((LEV, H, W)), shape((384, 128))],
        10**7,
        40,
        in_specs=[vmem] * 14,
        out_specs=[hbm, vmem],
        scratch_shapes=[
            rows(24), rows(24), rows(8), rows(8), rows(192, BF), rows(192, BF), rows(64, BF),
            rows(64), rows(64), rows(64), rows(32), rows(192, BF), rows(192, BF), rows(64, BF),
            rows(8), rows(8), rows(8), rows(8),
            pltpu.VMEM((64, 128), F32), pltpu.VMEM((64, 128), F32), pltpu.VMEM((32, 128), F32),
            pltpu.VMEM((64, 72), F32), pltpu.VMEM((64, 576), F32), pltpu.VMEM((32, 64), F32),
            pltpu.VMEM((LEV, H, W), F32), pltpu.SemaphoreType.DMA,
        ],
    )(init, target, mask, below, above, from_left, from_right, *weights)
    total = total_of(grad)
    u1, u2, u3 = kernel(finish, [shape(one.shape), shape(two.shape), shape(head.shape)], 10**6, 8)(
        total, d1, d2, d3, choose, below_ratio
    )
    return final, u1, u2, u3


def solution(mesh):
    count = mesh.shape["gy"] // 8
    torus = Mesh(mesh.devices.reshape(mesh.shape["gx"], count, 4, 2), ("gx", *GY))
    placed = (P(None, "gx", GY), P(None, "gx", GY), P("gx", GY), P(), P(), P(), P(), P(), P(), P())
    return jax.shard_map(
        per_device,
        mesh=torus,
        in_specs=placed,
        out_specs=(P(None, "gx", GY), P(), P(), P()),
        check_vma=False,
    )
```

```python
import math

import jax
import jax.numpy as jnp
from jax import lax
from jax.experimental import pallas as pl
from jax.experimental.pallas import tpu as pltpu
from jax.sharding import Mesh
from jax.sharding import PartitionSpec as P

LEV = 8
C = 64
K = 32
GROUPS = 6
PARAMS = 43680
GY = ("gy_0", "gy_1", "gy_2")
H = 8
W = 256
PITCH = 384
REACH = 6
BF = jnp.bfloat16
F32 = jnp.float32
NT = (((1,), (1,)), ((), ()))


def dot(a, b):
    return jnp.dot(a, b, preferred_element_type=F32)


def dot_nt(a, b):
    return lax.dot_general(a, b, NT, preferred_element_type=F32)


def turned(v, by):
    return pltpu.roll(v, by % v.shape[1], 1)


def sigmoid(v):
    return 0.5 * jnp.tanh(0.5 * v) + 0.5


def silu_slope(v, s):
    return s * (1.0 + v * (1.0 - s))


def pack_rows(own_ref, low_ref, high_ref):
    wet = own_ref[2 * LEV, :, :]
    low_ref[64:72, :] = wet
    high_ref[64:72, :] = wet
    for k in range(REACH):
        low_ref[k * 8 : k * 8 + 8, :] = own_ref[0:LEV, k, :] * wet[k : k + 1]
        r = H - REACH + k
        high_ref[k * 8 : k * 8 + 8, :] = own_ref[0:LEV, r, :] * wet[r : r + 1]
    for k in range(2):
        low_ref[48 + k * 8 : 56 + k * 8, :] = own_ref[LEV : 2 * LEV, k, :]
        high_ref[48 + k * 8 : 56 + k * 8, :] = own_ref[LEV : 2 * LEV, H - 2 + k, :]


def row_parts(r, own_ref, below_ref, above_ref):
    if 0 <= r < H:
        wet = own_ref[2 * LEV, r : r + 1, :]
        return own_ref[0:LEV, r, :] * wet, wet, own_ref[LEV : 2 * LEV, r, :]
    ref, k = (below_ref, r + REACH) if r < 0 else (above_ref, r - H)
    field = ref[k * 8 : k * 8 + 8, :]
    m = r + H if r < 0 else r - H
    wet = ref[64 + m : 65 + m, :]
    target = None
    if -2 <= r < H + 2:
        t = r + 2 if r < 0 else r - H
        target = ref[48 + 8 * t : 56 + 8 * t, :]
    return field, wet, target


def pack_cols(own_ref, below_ref, above_ref, left_ref, right_ref):
    lane = lax.broadcasted_iota(jnp.int32, (8, 128), 1)
    zero = jnp.zeros((8, 128), F32)
    packed = [zero] * 6
    for r in range(-REACH, H + REACH):
        field, wet, target = row_parts(r, own_ref, below_ref, above_ref)
        wet = jnp.broadcast_to(wet, (8, W))
        at, by = divmod(r + REACH, 8)
        inner = lane - 16 * by
        for side, first, moves in ((0, 0, (0, 6, 10)), (3, 128, (6, 10, 12))):
            move = [by * 16 + m for m in moves]
            v = turned(field[:, first : first + 128], move[0])
            v = jnp.where(inner < 6, v, turned(wet[:, first : first + 128], move[1]))
            if target is not None:
                v = jnp.where(inner < 10, v, turned(target[:, first : first + 128], move[2]))
            packed[side + at] = jnp.where((inner >= 0) & (inner < 12), v, packed[side + at])
    for k in range(3):
        left_ref[k * 8 : k * 8 + 8, :] = packed[k]
        right_ref[k * 8 : k * 8 + 8, :] = packed[3 + k]


def row_sums(parts):
    return jnp.concatenate([jnp.sum(v * v, axis=1, keepdims=True) for v in parts], axis=0)


def prepare(
    one_ref, two_ref, head_ref, d1_ref, d2_ref, d3_ref, gid_ref,
    w1_ref, w2_ref, w3_ref, w3t_ref, w2t_ref, w1t_ref, bias_ref, choose_ref, below_ref,
):
    one, two, head = one_ref[...], two_ref[...], head_ref[...]
    w1_ref[...] = one[:, : 9 * LEV].astype(BF)
    w2_ref[...] = jnp.concatenate(
        [
            jnp.concatenate(
                [two[:, (3 * a + b) * C : (3 * a + b + 1) * C] for a in range(3)], axis=1
            )
            for b in range(3)
        ],
        axis=0,
    ).astype(BF)
    w3_ref[...] = head[:, :C].astype(BF)
    w3t_ref[...] = head[:, :C].T.astype(BF)
    w2t_ref[...] = jnp.concatenate(
        [
            jnp.concatenate(
                [two[:, (8 - 3 * a - b) * C : (9 - 3 * a - b) * C].T for a in range(3)], axis=1
            )
            for b in range(3)
        ],
        axis=0,
    ).astype(BF)
    w1t_ref[...] = jnp.concatenate(
        [
            jnp.concatenate(
                [one[:, (3 * (2 - a) + b) * LEV : (3 * (2 - a) + b + 1) * LEV].T for a in range(3)],
                axis=1,
            )
            for b in range(3)
        ],
        axis=0,
    ).astype(BF)
    bias_ref[0:64, :] = jnp.broadcast_to(one[:, 9 * LEV :], (64, 128))
    bias_ref[64:128, :] = jnp.broadcast_to(two[:, 9 * C :], (64, 128))
    bias_ref[128:160, :] = jnp.broadcast_to(head[:, C:], (32, 128))
    group = lax.broadcasted_iota(jnp.int32, (128, 160), 0)
    choose = jnp.where(gid_ref[...] == group, 1.0, 0.0).T
    choose_ref[...] = choose
    sums = jnp.sum(choose * row_sums((d1_ref[...], d2_ref[...], d3_ref[...])), axis=0, keepdims=True)
    below_ref[...] = jnp.sqrt(sums + 1e-06)


def lanes(parts):
    return parts[0] if len(parts) == 1 else jnp.concatenate(parts, axis=1)


def cut(v, n):
    return [v[:, k * PITCH : (k + 1) * PITCH] for k in range(n)]


def folded(v):
    total = v[:, :128]
    for k in range(1, v.shape[1] // 128):
        total = total + v[:, k * 128 : (k + 1) * 128]
    return total


def main(
    own_ref, below_ref, above_ref, fromleft_ref, fromright_ref,
    w1_ref, w2_ref, w3_ref, w3t_ref, w2t_ref, w1t_ref, bias_ref,
    final_ref, grad_ref,
    xc0, xc1, wet_s, tgt, hm0, hm1, hc0, hc1, h2s, sp10, sp11, sp2, wd, em0, em1, e1s, rem, up, down, fin,
    b1g, b2g, b3g, g1, g2, g3, final_v, sem,
):
    lane = lax.broadcasted_iota(jnp.int32, (8, 128), 1)
    zero = jnp.zeros((8, 128), F32)
    for r in range(-REACH, H + REACH):
        field, wet, target = row_parts(r, own_ref, below_ref, above_ref)
        at = (r + REACH) * 8
        block, by = divmod(r + REACH, 8)
        fl = fromleft_ref[block * 8 : block * 8 + 8, :]
        fr = fromright_ref[block * 8 : block * 8 + 8, :]

        def rim(first, width):
            right = turned(fr, -(by * 16 + first))
            left = turned(fl, -(by * 16 + first) - width)
            return jnp.where(lane < width, right, jnp.where(lane >= 128 - width, left, zero))

        row = jnp.concatenate([field, rim(0, 6)], axis=1)
        xc0[at * 3 : at * 3 + 24, :] = jnp.concatenate(
            [turned(row, 1), row, turned(row, -1)], axis=0
        )
        wet_s[at : at + 8, :] = jnp.concatenate([jnp.broadcast_to(wet, (8, W)), rim(6, 4)], axis=1)
        if target is not None:
            tgt[at : at + 8, :] = jnp.concatenate([target, rim(10, 2)], axis=1)
    for ref in (b1g, b2g, b3g, g1, g2, g3):
        ref[...] = jnp.zeros(ref.shape, F32)
    for r in (4, 5, 14, 15):
        em0[r * 64 : r * 64 + 64, :] = jnp.zeros((64, PITCH), BF)

    col = lax.broadcasted_iota(jnp.int32, (1, PITCH), 1)
    col = jnp.where(col < 320, col, col - PITCH) + lax.axis_index(GY) * W
    col_in = jnp.where((col >= 0) & (col < lax.axis_size(GY) * W), 1.0, 0.0).astype(F32)

    row0 = lax.axis_index("gx") * H

    def inside(r):
        i = row0 + r - REACH
        return col_in * jnp.where((i >= 0) & (i < lax.axis_size("gx") * H), 1.0, 0.0)

    def bias(at, n):
        b = bias_ref[at : at + n, :]
        return jnp.concatenate([b] * 3, axis=1)

    def part(ref, r, size, first=0, count=None):
        start = r * size + first
        return ref.at[start : start + (size if count is None else count), :]

    def loop(lo, hi, per, body):
        for first in range(lo, hi, per):
            body([first + REACH + k for k in range(per)])

    def thrice(v):
        return turned(v, 1), v, turned(v, -1)

    def conv(weights, ref, rs):
        y = dot(weights, lanes([part(ref, r - 1, 64, 0, 192)[...] for r in rs]))
        return [
            turned(v[0:64], 1) + v[64:128] + turned(v[128:192], -1) for v in cut(y, len(rs))
        ]

    def first_layer(xc, hm, hc, sp1):
        def body(rs):
            x9 = lanes([part(xc, r - 1, 24, 0, 72)[...].astype(BF) for r in rs])
            for r, z in zip(rs, cut(dot(w1_ref[...], x9), len(rs))):
                z = z + bias(0, 64)
                s = sigmoid(z)
                keep = inside(r)
                h = (z * s * keep).astype(BF)
                part(hm, r, 64)[...] = h
                if -1 <= r - REACH <= H:
                    for k, piece in enumerate(thrice(h)):
                        part(hc, r, 192, 64 * k, 64)[...] = piece
                    part(sp1, r, 64)[...] = silu_slope(z, s) * keep

        return body

    def second_layer(hm, rs):
        h2, slope = [], []
        for z in conv(w2_ref[...], hm, rs):
            z = z + bias(64, 64)
            s = sigmoid(z)
            h2.append((z * s).astype(BF))
            slope.append(silu_slope(z, s))
        q = cut(dot(w3_ref[...], lanes(h2)), len(rs))
        return lanes(h2), lanes(slope), lanes([sigmoid(v + bias(128, 32)) for v in q])

    def slopes(xc, r):
        x = part(xc, r, 24, 8, 8)[...]
        beside = (
            part(xc, r + 1, 24, 8, 8)[...],
            part(xc, r - 1, 24, 8, 8)[...],
            part(xc, r, 24, 16, 8)[...],
            part(xc, r, 24, 0, 8)[...],
        )
        return x, [b - x for b in beside]

    def tail_zero(rs):
        h2, slope, p = second_layer(hm0, rs)
        n = len(rs)
        for r, h2r, sr, pr in zip(rs, cut(h2, n), cut(slope, n), cut(p, n)):
            part(h2s, r, 64)[...] = h2r
            part(sp2, r, 64)[...] = sr
            x, diff = slopes(xc0, r)
            wet = part(wet_s, r, 8)[...]
            change = jnp.zeros_like(x)
            for k in range(4):
                pk = pr[8 * k : 8 * k + 8]
                move = 0.25 * pk * diff[k]
                change = change + move
                part(wd, r, 32, 8 * k, 8)[...] = wet * move * (1.0 - pk)
            for k, piece in enumerate(thrice(x + wet * change)):
                part(xc1, r, 24, 8 * k, 8)[...] = piece

    def tail_grads(rs, e3, e2, h2, hc):
        b3g[...] += sum(folded(e[:, :W]) for e in e3)
        b2g[...] += sum(folded(e[:, :W]) for e in e2)
        g3[...] += dot_nt(
            lanes([e[:, :W].astype(BF) for e in e3]), lanes([v[:, :W] for v in h2])
        )
        g2[...] += dot_nt(
            lanes([part(hc, r - 1, 192, 0, 576)[:, :W] for r in rs]),
            lanes([e[:, :W].astype(BF) for e in e2]),
        )

    def tail_one(own):
        def body(rs):
            h2, slope, p = second_layer(hm1, rs)
            n = len(rs)
            e3s = []
            for r, pr in zip(rs, cut(p, n)):
                x, diff = slopes(xc1, r)
                wet = part(wet_s, r, 8)[...]
                c = [0.25 * pr[8 * k : 8 * k + 8] for k in range(4)]
                move = [c[k] * diff[k] for k in range(4)]
                new = x + wet * (move[0] + move[1] + move[2] + move[3])
                if own:
                    part(fin, r, 8)[...] = new
                g = wet * (new - part(tgt, r, 8)[...])
                wg = wet * g
                t = [wg * c[k] for k in range(4)]
                left = g - t[0] - t[1] - t[2] - t[3]
                part(rem, r, 8)[...] = left + turned(t[2], 1) + turned(t[3], -1)
                part(up, r, 8)[...] = t[0]
                part(down, r, 8)[...] = t[1]
                e3s.append(
                    jnp.concatenate(
                        [wg * move[k] * (1.0 - pr[8 * k : 8 * k + 8]) for k in range(4)], axis=0
                    )
                )
            e2 = dot(w3t_ref[...], lanes([e.astype(BF) for e in e3s])) * slope
            e2s = cut(e2, n)
            for r, e in zip(rs, e2s):
                part(em1, r, 64)[...] = e.astype(BF)
            if own:
                tail_grads(rs, e3s, e2s, cut(h2, n), hc1)

        return body

    def first_error(em, sp1, rs):
        return [v * part(sp1, r, 64)[...] for r, v in zip(rs, conv(w2t_ref[...], em, rs))]

    def first_grads(rs, e1, xc, width):
        b1g[...] += sum(folded(e[:, :width]) for e in e1)
        g1[...] += dot_nt(
            lanes([e[:, :width].astype(BF) for e in e1]),
            lanes([part(xc, r - 1, 24, 0, 72)[:, :width].astype(BF) for r in rs]),
        )

    def first_one(own):
        def body(rs):
            e1 = first_error(em1, sp11, rs)
            for r, e in zip(rs, e1):
                part(e1s, r, 64)[...] = e.astype(BF)
            if own:
                first_grads(rs, e1, xc1, W)

        return body

    def back_zero(rs):
        y = dot(w1t_ref[...], lanes([part(e1s, r - 1, 64, 0, 192)[...] for r in rs]))
        e3s = []
        for r, yr in zip(rs, cut(y, len(rs))):
            g = part(rem, r, 8)[...] + part(up, r - 1, 8)[...] + part(down, r + 1, 8)[...]
            g = g + yr[8:16] + turned(yr[0:8], -1) + turned(yr[16:24], 1)
            e3 = jnp.concatenate([g] * 4, axis=0) * part(wd, r, 32)[...]
            e3s.append(jnp.concatenate([e3[:, :W], jnp.zeros((K, PITCH - W), F32)], axis=1))
        e2 = dot(w3t_ref[...], lanes([e.astype(BF) for e in e3s]))
        e2s = [v * part(sp2, r, 64)[...] for r, v in zip(rs, cut(e2, len(rs)))]
        for r, e in zip(rs, e2s):
            part(em0, r, 64)[...] = e.astype(BF)
        tail_grads(rs, e3s, e2s, [part(h2s, r, 64)[...] for r in rs], hc0)

    def first_zero(rs):
        first_grads(rs, first_error(em0, sp10, rs), xc0, PITCH)

    loop(-5, 13, 9, first_layer(xc0, hm0, hc0, sp10))
    loop(-4, 12, 16, tail_zero)
    loop(-3, 11, 14, first_layer(xc1, hm1, hc1, sp11))
    tail_one(False)([4, 5, 14, 15])
    loop(0, 8, 8, tail_one(True))
    for r in range(H):
        final_v[:, r, :] = fin[(r + REACH) * 8 : (r + REACH) * 8 + 8, :W]
    out = pltpu.make_async_copy(final_v, final_ref, sem)
    out.start()
    first_one(False)([5, 14])
    loop(0, 8, 8, first_one(True))
    loop(0, 8, 8, back_zero)
    loop(-1, 9, 10, first_zero)

    grad_ref[0:256, :] = jnp.concatenate([g2[0:256, :], g2[256:512, :]], axis=1)
    grad_ref[256:320, :] = jnp.concatenate([g2[512:576, :], g1[:, 0:64]], axis=1)
    sums = [jnp.sum(ref[...], axis=1, keepdims=True) for ref in (b1g, b2g, b3g)]
    sums[2] = jnp.concatenate([sums[2], jnp.zeros((32, 1), F32)], axis=0)
    grad_ref[320:384, :] = jnp.concatenate(
        [
            g1[:, 64:72],
            *sums,
            jnp.zeros((64, 53), F32),
            jnp.concatenate([g3[...], jnp.zeros((32, 64), F32)], axis=0),
        ],
        axis=1,
    )
    out.wait()


def finish(total_ref, d1_ref, d2_ref, d3_ref, choose_ref, below_ref, u1_ref, u2_ref, u3_ref):
    t = [total_ref[k * 64 : k * 64 + 64, :] for k in range(6)]
    two = jnp.concatenate([v[:, :64].T for v in t[:4]] + [v[:, 64:].T for v in t[:4]] + [t[4][:, :64].T, t[5][:, 9:10]], axis=1)
    one = jnp.concatenate([t[4][:, 64:], t[5][:, :8], t[5][:, 8:9]], axis=1)
    three = jnp.concatenate([t[5][:32, 64:], t[5][:32, 10:11]], axis=1)
    grads = (one, two, three)
    squares = row_sums(grads)
    norm = jnp.sqrt(jnp.sum(squares, axis=0, keepdims=True))
    factor = 1.0 / jnp.maximum(norm, 1.0)
    clipped = [v * factor for v in grads]
    choose = choose_ref[...]
    ratios = factor * jnp.sqrt(jnp.sum(choose * squares, axis=0, keepdims=True)) / below_ref[...]
    row_ratio = jnp.sum(choose * ratios, axis=1, keepdims=True)
    scaling = math.sqrt(PARAMS)
    at = 0
    for ref, v, d_ref in zip((u1_ref, u2_ref, u3_ref), clipped, (d1_ref, d2_ref, d3_ref)):
        n = v.shape[0]
        ref[...] = scaling * (v + row_ratio[at : at + n] * d_ref[...])
        at += n


def shape(dims, dtype=F32):
    return jax.ShapeDtypeStruct(dims, dtype)


def kernel(body, outs, cost, mib, **more):
    return pl.pallas_call(
        body,
        out_shape=outs,
        cost_estimate=pl.CostEstimate(flops=cost, bytes_accessed=cost, transcendentals=0),
        compiler_params=pltpu.CompilerParams(vmem_limit_bytes=mib * 2**20),
        **more,
    )


def exchange(forward, backward, axis):
    count = lax.axis_size(axis)
    ahead = [(i, i + 1) for i in range(count - 1)]
    back = [(b, a) for a, b in ahead]
    return lax.ppermute(forward, axis, ahead), lax.ppermute(backward, axis, back)


def total_of(grad):
    near = ("gy_0", "gy_1")
    n = lax.axis_size(near)
    pieces = grad.reshape(n, -1, 128)
    own = jnp.sum(lax.all_to_all(pieces, near, 0, 0, tiled=True), axis=0)
    own = own + lax.ppermute(own, "gy_2", [(0, 1), (1, 0)])
    m = lax.axis_size("gx")
    copies = jnp.broadcast_to(own, (m, *own.shape))
    own = jnp.sum(lax.all_to_all(copies, "gx", 0, 0, tiled=True), axis=0)
    copies = jnp.broadcast_to(own, (n, *own.shape))
    return lax.all_to_all(copies, near, 0, 0, tiled=True).reshape(grad.shape)


def per_device(init, target, mask, one, two, head, d1, d2, d3, gid):
    hbm = pl.BlockSpec(memory_space=pltpu.HBM)
    vmem = pl.BlockSpec(memory_space=pltpu.VMEM)
    def widened(v, first):
        return jnp.pad(v, ((first, 2 * LEV + 1 - first - v.shape[0]), (0, 0), (0, 0)))

    own = widened(init, 0) + widened(target, LEV) + widened(mask[None], 2 * LEV).astype(F32)
    to_low, to_high = kernel(pack_rows, [shape((72, W))] * 2, 10**5, 4)(own)
    below, above = exchange(to_high, to_low, "gx")
    to_left, to_right = kernel(pack_cols, [shape((24, 128))] * 2, 10**5, 4)(
        own, below, above
    )
    from_left, from_right = exchange(to_right, to_left, GY)
    *weights, choose, below_ratio = kernel(
        prepare,
        [
            shape((C, 72), BF), shape((192, 192), BF), shape((K, C), BF), shape((C, K), BF),
            shape((192, 192), BF), shape((24, 192), BF), shape((160, 128)),
            shape((160, 128)), shape((1, 128)),
        ],
        10**6,
        8,
    )(one, two, head, d1, d2, d3, gid.reshape(1, -1))

    def rows(size, dtype=F32):
        return pltpu.VMEM((20 * size, PITCH), dtype)

    final, grad = kernel(
        main,
        [shape((LEV, H, W)), shape((384, 128))],
        10**7,
        40,
        in_specs=[vmem] * 12,
        out_specs=[hbm, vmem],
        scratch_shapes=[
            rows(24), rows(24), rows(8), rows(8), rows(64, BF), rows(64, BF), rows(192, BF), rows(192, BF), rows(64, BF),
            rows(64), rows(64), rows(64), rows(32), rows(64, BF), rows(64, BF), rows(64, BF),
            rows(8), rows(8), rows(8), rows(8),
            pltpu.VMEM((64, 128), F32), pltpu.VMEM((64, 128), F32), pltpu.VMEM((32, 128), F32),
            pltpu.VMEM((64, 72), F32), pltpu.VMEM((576, 64), F32), pltpu.VMEM((32, 64), F32),
            pltpu.VMEM((LEV, H, W), F32), pltpu.SemaphoreType.DMA,
        ],
    )(own, below, above, from_left, from_right, *weights)
    total = total_of(grad)
    u1, u2, u3 = kernel(finish, [shape(one.shape), shape(two.shape), shape(head.shape)], 10**6, 8)(
        total, d1, d2, d3, choose, below_ratio
    )
    return final, u1, u2, u3


def solution(mesh):
    count = mesh.shape["gy"] // 8
    torus = Mesh(mesh.devices.reshape(mesh.shape["gx"], count, 4, 2), ("gx", *GY))
    placed = (P(None, "gx", GY), P(None, "gx", GY), P("gx", GY), P(), P(), P(), P(), P(), P(), P())
    return jax.shard_map(
        per_device,
        mesh=torus,
        in_specs=placed,
        out_specs=(P(None, "gx", GY), P(), P(), P()),
        check_vma=False,
    )
```

```python
import math

import jax
import jax.numpy as jnp
from jax import lax
from jax.experimental import pallas as pl
from jax.experimental.pallas import tpu as pltpu
from jax.sharding import Mesh
from jax.sharding import PartitionSpec as P

LEV = 8
C = 64
K = 32
GROUPS = 6
PARAMS = 43680
GY = ("gy_0", "gy_1", "gy_2")
H = 8
W = 256
PITCH = 384
REACH = 6
BF = jnp.bfloat16
F32 = jnp.float32
NT = (((1,), (1,)), ((), ()))


def dot(a, b):
    return jnp.dot(a, b, preferred_element_type=F32)


def dot_nt(a, b):
    return lax.dot_general(a, b, NT, preferred_element_type=F32)


def turned(v, by):
    return pltpu.roll(v, by % v.shape[1], 1)


def sigmoid(v):
    return 0.5 * jnp.tanh(0.5 * v) + 0.5


def silu_slope(v, s):
    return s * (1.0 + v * (1.0 - s))


def pack_rows(own_ref, first_ref, second_ref):
    even = is_even("gx")
    wet = own_ref[2 * LEV, :, :]

    def put(at, low, high):
        first_ref[at : at + 8, :] = jnp.where(even, high, low)
        second_ref[at : at + 8, :] = jnp.where(even, low, high)

    put(64, wet, wet)
    for k in range(REACH):
        r = H - REACH + k
        put(k * 8, own_ref[0:LEV, k, :] * wet[k : k + 1], own_ref[0:LEV, r, :] * wet[r : r + 1])
    for k in range(2):
        put(48 + k * 8, own_ref[LEV : 2 * LEV, k, :], own_ref[LEV : 2 * LEV, H - 2 + k, :])


def is_even(axis):
    return lax.rem(lax.axis_index(axis), 2) == 0


class Chosen:
    def __init__(self, condition, first, second):
        self.condition, self.first, self.second = condition, first, second

    def __getitem__(self, index):
        return jnp.where(self.condition, self.first[index], self.second[index])


def by_side(axis, first_ref, second_ref):
    even = is_even(axis)
    return Chosen(even, second_ref, first_ref), Chosen(even, first_ref, second_ref)


def row_parts(r, own_ref, below_ref, above_ref):
    if 0 <= r < H:
        wet = own_ref[2 * LEV, r : r + 1, :]
        return own_ref[0:LEV, r, :] * wet, wet, own_ref[LEV : 2 * LEV, r, :]
    ref, k = (below_ref, r + REACH) if r < 0 else (above_ref, r - H)
    field = ref[k * 8 : k * 8 + 8, :]
    m = r + H if r < 0 else r - H
    wet = ref[64 + m : 65 + m, :]
    target = None
    if -2 <= r < H + 2:
        t = r + 2 if r < 0 else r - H
        target = ref[48 + 8 * t : 56 + 8 * t, :]
    return field, wet, target


def pack_cols(own_ref, swap_one_ref, swap_two_ref, first_ref, second_ref):
    below_ref, above_ref = by_side("gx", swap_one_ref, swap_two_ref)
    even = is_even(GY)
    lane = lax.broadcasted_iota(jnp.int32, (8, 128), 1)
    zero = jnp.zeros((8, 128), F32)
    packed = [zero] * 6
    for r in range(-REACH, H + REACH):
        field, wet, target = row_parts(r, own_ref, below_ref, above_ref)
        wet = jnp.broadcast_to(wet, (8, W))
        at, by = divmod(r + REACH, 8)
        inner = lane - 16 * by
        for side, first, moves in ((0, 0, (0, 6, 10)), (3, 128, (6, 10, 12))):
            move = [by * 16 + m for m in moves]
            v = turned(field[:, first : first + 128], move[0])
            v = jnp.where(inner < 6, v, turned(wet[:, first : first + 128], move[1]))
            if target is not None:
                v = jnp.where(inner < 10, v, turned(target[:, first : first + 128], move[2]))
            packed[side + at] = jnp.where((inner >= 0) & (inner < 12), v, packed[side + at])
    for k in range(3):
        first_ref[k * 8 : k * 8 + 8, :] = jnp.where(even, packed[3 + k], packed[k])
        second_ref[k * 8 : k * 8 + 8, :] = jnp.where(even, packed[k], packed[3 + k])


def row_sums(parts):
    return jnp.concatenate([jnp.sum(v * v, axis=1, keepdims=True) for v in parts], axis=0)


def prepare(
    one_ref, two_ref, head_ref, d1_ref, d2_ref, d3_ref, gid_ref,
    w1_ref, w2_ref, w3_ref, w3t_ref, w2t_ref, w1t_ref, bias_ref, choose_ref, below_ref,
):
    one, two, head = one_ref[...], two_ref[...], head_ref[...]
    w1_ref[...] = one[:, : 9 * LEV].astype(BF)
    w2_ref[...] = jnp.concatenate(
        [
            jnp.concatenate(
                [two[:, (3 * a + b) * C : (3 * a + b + 1) * C] for a in range(3)], axis=1
            )
            for b in range(3)
        ],
        axis=0,
    ).astype(BF)
    w3_ref[...] = head[:, :C].astype(BF)
    w3t_ref[...] = head[:, :C].T.astype(BF)
    w2t_ref[...] = jnp.concatenate(
        [
            jnp.concatenate(
                [two[:, (8 - 3 * a - b) * C : (9 - 3 * a - b) * C].T for a in range(3)], axis=1
            )
            for b in range(3)
        ],
        axis=0,
    ).astype(BF)
    w1t_ref[...] = jnp.concatenate(
        [
            jnp.concatenate(
                [one[:, (3 * (2 - a) + b) * LEV : (3 * (2 - a) + b + 1) * LEV].T for a in range(3)],
                axis=1,
            )
            for b in range(3)
        ],
        axis=0,
    ).astype(BF)
    bias_ref[0:64, :] = jnp.broadcast_to(one[:, 9 * LEV :], (64, 128))
    bias_ref[64:128, :] = jnp.broadcast_to(two[:, 9 * C :], (64, 128))
    bias_ref[128:160, :] = jnp.broadcast_to(head[:, C:], (32, 128))
    group = lax.broadcasted_iota(jnp.int32, (128, 160), 0)
    choose = jnp.where(gid_ref[...] == group, 1.0, 0.0).T
    choose_ref[...] = choose
    sums = jnp.sum(choose * row_sums((d1_ref[...], d2_ref[...], d3_ref[...])), axis=0, keepdims=True)
    below_ref[...] = jnp.sqrt(sums + 1e-06)


def lanes(parts):
    return parts[0] if len(parts) == 1 else jnp.concatenate(parts, axis=1)


def cut(v, n):
    return [v[:, k * PITCH : (k + 1) * PITCH] for k in range(n)]


def folded(v):
    total = v[:, :128]
    for k in range(1, v.shape[1] // 128):
        total = total + v[:, k * 128 : (k + 1) * 128]
    return total


def main(
    own_ref, row_one_ref, row_two_ref, col_one_ref, col_two_ref,
    w1_ref, w2_ref, w3_ref, w3t_ref, w2t_ref, w1t_ref, bias_ref,
    final_ref, grad_ref,
    xc0, xc1, wet_s, tgt, hm0, hm1, hc0, hc1, h2s, sp10, sp11, sp2, wd, em0, em1, e1s, rem, up, down, fin,
    b1g, b2g, b3g, g1, g2, g3, final_v, sem,
):
    below_ref, above_ref = by_side("gx", row_one_ref, row_two_ref)
    fromleft_ref, fromright_ref = by_side(GY, col_one_ref, col_two_ref)
    lane = lax.broadcasted_iota(jnp.int32, (8, 128), 1)
    zero = jnp.zeros((8, 128), F32)
    for r in range(-REACH, H + REACH):
        field, wet, target = row_parts(r, own_ref, below_ref, above_ref)
        at = (r + REACH) * 8
        block, by = divmod(r + REACH, 8)
        fl = fromleft_ref[block * 8 : block * 8 + 8, :]
        fr = fromright_ref[block * 8 : block * 8 + 8, :]

        def rim(first, width):
            right = turned(fr, -(by * 16 + first))
            left = turned(fl, -(by * 16 + first) - width)
            return jnp.where(lane < width, right, jnp.where(lane >= 128 - width, left, zero))

        row = jnp.concatenate([field, rim(0, 6)], axis=1)
        xc0[at * 3 : at * 3 + 24, :] = jnp.concatenate(
            [turned(row, 1), row, turned(row, -1)], axis=0
        )
        wet_s[at : at + 8, :] = jnp.concatenate([jnp.broadcast_to(wet, (8, W)), rim(6, 4)], axis=1)
        if target is not None:
            tgt[at : at + 8, :] = jnp.concatenate([target, rim(10, 2)], axis=1)
    for ref in (b1g, b2g, b3g, g1, g2, g3):
        ref[...] = jnp.zeros(ref.shape, F32)
    for r in (4, 5, 14, 15):
        em0[r * 64 : r * 64 + 64, :] = jnp.zeros((64, PITCH), BF)

    col = lax.broadcasted_iota(jnp.int32, (1, PITCH), 1)
    col = jnp.where(col < 320, col, col - PITCH) + lax.axis_index(GY) * W
    col_in = jnp.where((col >= 0) & (col < lax.axis_size(GY) * W), 1.0, 0.0).astype(F32)

    row0 = lax.axis_index("gx") * H

    def inside(r):
        i = row0 + r - REACH
        return col_in * jnp.where((i >= 0) & (i < lax.axis_size("gx") * H), 1.0, 0.0)

    def bias(at, n):
        b = bias_ref[at : at + n, :]
        return jnp.concatenate([b] * 3, axis=1)

    def part(ref, r, size, first=0, count=None):
        start = r * size + first
        return ref.at[start : start + (size if count is None else count), :]

    def loop(lo, hi, per, body):
        for first in range(lo, hi, per):
            body([first + REACH + k for k in range(per)])

    def thrice(v):
        return turned(v, 1), v, turned(v, -1)

    def conv(weights, ref, rs):
        y = dot(weights, lanes([part(ref, r - 1, 64, 0, 192)[...] for r in rs]))
        return [
            turned(v[0:64], 1) + v[64:128] + turned(v[128:192], -1) for v in cut(y, len(rs))
        ]

    def first_layer(xc, hm, hc, sp1):
        def body(rs):
            x9 = lanes([part(xc, r - 1, 24, 0, 72)[...].astype(BF) for r in rs])
            for r, z in zip(rs, cut(dot(w1_ref[...], x9), len(rs))):
                z = z + bias(0, 64)
                s = sigmoid(z)
                keep = inside(r)
                h = (z * s * keep).astype(BF)
                part(hm, r, 64)[...] = h
                if -1 <= r - REACH <= H:
                    for k, piece in enumerate(thrice(h)):
                        part(hc, r, 192, 64 * k, 64)[...] = piece
                    part(sp1, r, 64)[...] = silu_slope(z, s) * keep

        return body

    def second_layer(hm, rs):
        h2, slope = [], []
        for z in conv(w2_ref[...], hm, rs):
            z = z + bias(64, 64)
            s = sigmoid(z)
            h2.append((z * s).astype(BF))
            slope.append(silu_slope(z, s))
        q = cut(dot(w3_ref[...], lanes(h2)), len(rs))
        return lanes(h2), lanes(slope), lanes([sigmoid(v + bias(128, 32)) for v in q])

    def slopes(xc, r):
        x = part(xc, r, 24, 8, 8)[...]
        beside = (
            part(xc, r + 1, 24, 8, 8)[...],
            part(xc, r - 1, 24, 8, 8)[...],
            part(xc, r, 24, 16, 8)[...],
            part(xc, r, 24, 0, 8)[...],
        )
        return x, [b - x for b in beside]

    def tail_zero(rs):
        h2, slope, p = second_layer(hm0, rs)
        n = len(rs)
        for r, h2r, sr, pr in zip(rs, cut(h2, n), cut(slope, n), cut(p, n)):
            part(h2s, r, 64)[...] = h2r
            part(sp2, r, 64)[...] = sr
            x, diff = slopes(xc0, r)
            wet = part(wet_s, r, 8)[...]
            change = jnp.zeros_like(x)
            for k in range(4):
                pk = pr[8 * k : 8 * k + 8]
                move = 0.25 * pk * diff[k]
                change = change + move
                part(wd, r, 32, 8 * k, 8)[...] = wet * move * (1.0 - pk)
            for k, piece in enumerate(thrice(x + wet * change)):
                part(xc1, r, 24, 8 * k, 8)[...] = piece

    def tail_grads(rs, e3, e2, h2, hc):
        b3g[...] += sum(folded(e[:, :W]) for e in e3)
        b2g[...] += sum(folded(e[:, :W]) for e in e2)
        g3[...] += dot_nt(
            lanes([e[:, :W].astype(BF) for e in e3]), lanes([v[:, :W] for v in h2])
        )
        g2[...] += dot_nt(
            lanes([part(hc, r - 1, 192, 0, 576)[:, :W] for r in rs]),
            lanes([e[:, :W].astype(BF) for e in e2]),
        )

    def tail_one(own):
        def body(rs):
            h2, slope, p = second_layer(hm1, rs)
            n = len(rs)
            e3s = []
            for r, pr in zip(rs, cut(p, n)):
                x, diff = slopes(xc1, r)
                wet = part(wet_s, r, 8)[...]
                c = [0.25 * pr[8 * k : 8 * k + 8] for k in range(4)]
                move = [c[k] * diff[k] for k in range(4)]
                new = x + wet * (move[0] + move[1] + move[2] + move[3])
                if own:
                    part(fin, r, 8)[...] = new
                g = wet * (new - part(tgt, r, 8)[...])
                wg = wet * g
                t = [wg * c[k] for k in range(4)]
                left = g - t[0] - t[1] - t[2] - t[3]
                part(rem, r, 8)[...] = left + turned(t[2], 1) + turned(t[3], -1)
                part(up, r, 8)[...] = t[0]
                part(down, r, 8)[...] = t[1]
                e3s.append(
                    jnp.concatenate(
                        [wg * move[k] * (1.0 - pr[8 * k : 8 * k + 8]) for k in range(4)], axis=0
                    )
                )
            e2 = dot(w3t_ref[...], lanes([e.astype(BF) for e in e3s])) * slope
            e2s = cut(e2, n)
            for r, e in zip(rs, e2s):
                part(em1, r, 64)[...] = e.astype(BF)
            if own:
                tail_grads(rs, e3s, e2s, cut(h2, n), hc1)

        return body

    def first_error(em, sp1, rs):
        return [v * part(sp1, r, 64)[...] for r, v in zip(rs, conv(w2t_ref[...], em, rs))]

    def first_grads(rs, e1, xc, width):
        b1g[...] += sum(folded(e[:, :width]) for e in e1)
        g1[...] += dot_nt(
            lanes([e[:, :width].astype(BF) for e in e1]),
            lanes([part(xc, r - 1, 24, 0, 72)[:, :width].astype(BF) for r in rs]),
        )

    def first_one(own):
        def body(rs):
            e1 = first_error(em1, sp11, rs)
            for r, e in zip(rs, e1):
                part(e1s, r, 64)[...] = e.astype(BF)
            if own:
                first_grads(rs, e1, xc1, W)

        return body

    def back_zero(rs):
        y = dot(w1t_ref[...], lanes([part(e1s, r - 1, 64, 0, 192)[...] for r in rs]))
        e3s = []
        for r, yr in zip(rs, cut(y, len(rs))):
            g = part(rem, r, 8)[...] + part(up, r - 1, 8)[...] + part(down, r + 1, 8)[...]
            g = g + yr[8:16] + turned(yr[0:8], -1) + turned(yr[16:24], 1)
            e3 = jnp.concatenate([g] * 4, axis=0) * part(wd, r, 32)[...]
            e3s.append(jnp.concatenate([e3[:, :W], jnp.zeros((K, PITCH - W), F32)], axis=1))
        e2 = dot(w3t_ref[...], lanes([e.astype(BF) for e in e3s]))
        e2s = [v * part(sp2, r, 64)[...] for r, v in zip(rs, cut(e2, len(rs)))]
        for r, e in zip(rs, e2s):
            part(em0, r, 64)[...] = e.astype(BF)
        tail_grads(rs, e3s, e2s, [part(h2s, r, 64)[...] for r in rs], hc0)

    def first_zero(rs):
        first_grads(rs, first_error(em0, sp10, rs), xc0, PITCH)

    loop(-5, 13, 9, first_layer(xc0, hm0, hc0, sp10))
    loop(-4, 12, 16, tail_zero)
    loop(-3, 11, 14, first_layer(xc1, hm1, hc1, sp11))
    tail_one(False)([4, 5, 14, 15])
    loop(0, 8, 8, tail_one(True))
    for r in range(H):
        final_v[:, r, :] = fin[(r + REACH) * 8 : (r + REACH) * 8 + 8, :W]
    out = pltpu.make_async_copy(final_v, final_ref, sem)
    out.start()
    first_one(False)([5, 14])
    loop(0, 8, 8, first_one(True))
    loop(0, 8, 8, back_zero)
    loop(-1, 9, 10, first_zero)

    grad_ref[0:256, :] = jnp.concatenate([g2[0:256, :], g2[256:512, :]], axis=1)
    grad_ref[256:320, :] = jnp.concatenate([g2[512:576, :], g1[:, 0:64]], axis=1)
    sums = [jnp.sum(ref[...], axis=1, keepdims=True) for ref in (b1g, b2g, b3g)]
    sums[2] = jnp.concatenate([sums[2], jnp.zeros((32, 1), F32)], axis=0)
    grad_ref[320:384, :] = jnp.concatenate(
        [
            g1[:, 64:72],
            *sums,
            jnp.zeros((64, 53), F32),
            jnp.concatenate([g3[...], jnp.zeros((32, 64), F32)], axis=0),
        ],
        axis=1,
    )
    out.wait()


def finish(total_ref, d1_ref, d2_ref, d3_ref, choose_ref, below_ref, u1_ref, u2_ref, u3_ref):
    t = [total_ref[k * 64 : k * 64 + 64, :] for k in range(6)]
    two = jnp.concatenate([v[:, :64].T for v in t[:4]] + [v[:, 64:].T for v in t[:4]] + [t[4][:, :64].T, t[5][:, 9:10]], axis=1)
    one = jnp.concatenate([t[4][:, 64:], t[5][:, :8], t[5][:, 8:9]], axis=1)
    three = jnp.concatenate([t[5][:32, 64:], t[5][:32, 10:11]], axis=1)
    grads = (one, two, three)
    squares = row_sums(grads)
    norm = jnp.sqrt(jnp.sum(squares, axis=0, keepdims=True))
    factor = 1.0 / jnp.maximum(norm, 1.0)
    clipped = [v * factor for v in grads]
    choose = choose_ref[...]
    ratios = factor * jnp.sqrt(jnp.sum(choose * squares, axis=0, keepdims=True)) / below_ref[...]
    row_ratio = jnp.sum(choose * ratios, axis=1, keepdims=True)
    scaling = math.sqrt(PARAMS)
    at = 0
    for ref, v, d_ref in zip((u1_ref, u2_ref, u3_ref), clipped, (d1_ref, d2_ref, d3_ref)):
        n = v.shape[0]
        ref[...] = scaling * (v + row_ratio[at : at + n] * d_ref[...])
        at += n


def shape(dims, dtype=F32):
    return jax.ShapeDtypeStruct(dims, dtype)


def kernel(body, outs, cost, mib, **more):
    return pl.pallas_call(
        body,
        out_shape=outs,
        cost_estimate=pl.CostEstimate(flops=cost, bytes_accessed=cost, transcendentals=0),
        compiler_params=pltpu.CompilerParams(vmem_limit_bytes=mib * 2**20),
        **more,
    )


def exchange(first, second, axis):
    count = lax.axis_size(axis)
    pairs = [[(i, i + 1) for i in range(start, count - 1, 2)] for start in (0, 1)]
    swaps = [[*p, *((b, a) for a, b in p)] for p in pairs]
    return lax.ppermute(first, axis, swaps[0]), lax.ppermute(second, axis, swaps[1])


def total_of(grad):
    near = ("gy_0", "gy_1")
    n = lax.axis_size(near)
    pieces = grad.reshape(n, -1, 128)
    own = jnp.sum(lax.all_to_all(pieces, near, 0, 0, tiled=True), axis=0)
    own = own + lax.ppermute(own, "gy_2", [(0, 1), (1, 0)])
    m = lax.axis_size("gx")
    copies = jnp.broadcast_to(own, (m, *own.shape))
    own = jnp.sum(lax.all_to_all(copies, "gx", 0, 0, tiled=True), axis=0)
    copies = jnp.broadcast_to(own, (n, *own.shape))
    return lax.all_to_all(copies, near, 0, 0, tiled=True).reshape(grad.shape)


def per_device(init, target, mask, one, two, head, d1, d2, d3, gid):
    hbm = pl.BlockSpec(memory_space=pltpu.HBM)
    vmem = pl.BlockSpec(memory_space=pltpu.VMEM)
    def widened(v, first):
        return jnp.pad(v, ((first, 2 * LEV + 1 - first - v.shape[0]), (0, 0), (0, 0)))

    own = widened(init, 0) + widened(target, LEV) + widened(mask[None], 2 * LEV).astype(F32)
    packs = kernel(pack_rows, [shape((72, W))] * 2, 10**5, 4)(own)
    rows_in = exchange(*packs, "gx")
    packs = kernel(pack_cols, [shape((24, 128))] * 2, 10**5, 4)(
        own, *rows_in
    )
    cols_in = exchange(*packs, GY)
    *weights, choose, below_ratio = kernel(
        prepare,
        [
            shape((C, 72), BF), shape((192, 192), BF), shape((K, C), BF), shape((C, K), BF),
            shape((192, 192), BF), shape((24, 192), BF), shape((160, 128)),
            shape((160, 128)), shape((1, 128)),
        ],
        10**6,
        8,
    )(one, two, head, d1, d2, d3, gid.reshape(1, -1))

    def rows(size, dtype=F32):
        return pltpu.VMEM((20 * size, PITCH), dtype)

    final, grad = kernel(
        main,
        [shape((LEV, H, W)), shape((384, 128))],
        10**7,
        40,
        in_specs=[vmem] * 12,
        out_specs=[hbm, vmem],
        scratch_shapes=[
            rows(24), rows(24), rows(8), rows(8), rows(64, BF), rows(64, BF), rows(192, BF), rows(192, BF), rows(64, BF),
            rows(64), rows(64), rows(64), rows(32), rows(64, BF), rows(64, BF), rows(64, BF),
            rows(8), rows(8), rows(8), rows(8),
            pltpu.VMEM((64, 128), F32), pltpu.VMEM((64, 128), F32), pltpu.VMEM((32, 128), F32),
            pltpu.VMEM((64, 72), F32), pltpu.VMEM((576, 64), F32), pltpu.VMEM((32, 64), F32),
            pltpu.VMEM((LEV, H, W), F32), pltpu.SemaphoreType.DMA,
        ],
    )(own, *rows_in, *cols_in, *weights)
    total = total_of(grad)
    u1, u2, u3 = kernel(finish, [shape(one.shape), shape(two.shape), shape(head.shape)], 10**6, 8)(
        total, d1, d2, d3, choose, below_ratio
    )
    return final, u1, u2, u3


def solution(mesh):
    count = mesh.shape["gy"] // 8
    torus = Mesh(mesh.devices.reshape(mesh.shape["gx"], count, 4, 2), ("gx", *GY))
    placed = (P(None, "gx", GY), P(None, "gx", GY), P("gx", GY), P(), P(), P(), P(), P(), P(), P())
    return jax.shard_map(
        per_device,
        mesh=torus,
        in_specs=placed,
        out_specs=(P(None, "gx", GY), P(), P(), P()),
        check_vma=False,
    )
```

```python
import math

import jax
import jax.numpy as jnp
from jax import lax
from jax.experimental import pallas as pl
from jax.experimental.pallas import tpu as pltpu
from jax.sharding import Mesh
from jax.sharding import PartitionSpec as P

LEV = 8
C = 64
K = 32
GROUPS = 6
PARAMS = 43680
GY = ("gy_0", "gy_1", "gy_2")
H = 8
W = 256
PITCH = 384
REACH = 6
BF = jnp.bfloat16
F32 = jnp.float32
NT = (((1,), (1,)), ((), ()))


def dot(a, b):
    return jnp.dot(a, b, preferred_element_type=F32)


def dot_nt(a, b):
    return lax.dot_general(a, b, NT, preferred_element_type=F32)


def turned(v, by):
    return pltpu.roll(v, by % v.shape[1], 1)


def sigmoid(v):
    return 0.5 * jnp.tanh(0.5 * v) + 0.5


def silu_slope(v, s):
    return s * (1.0 + v * (1.0 - s))


def pack_rows(own_ref, first_ref, second_ref):
    upward = first_is_higher("gx")
    wet = own_ref[2 * LEV, :, :]

    def put(at, low, high):
        first_ref[at : at + 8, :] = jnp.where(upward, high, low)
        second_ref[at : at + 8, :] = jnp.where(upward, low, high)

    put(64, wet, wet)
    for k in range(REACH):
        r = H - REACH + k
        put(k * 8, own_ref[0:LEV, k, :] * wet[k : k + 1], own_ref[0:LEV, r, :] * wet[r : r + 1])
    for k in range(2):
        put(48 + k * 8, own_ref[LEV : 2 * LEV, k, :], own_ref[LEV : 2 * LEV, H - 2 + k, :])


FIRST_SWAP = {"gx": 0, GY: 1}


def first_is_higher(axis):
    return lax.rem(lax.axis_index(axis), 2) == FIRST_SWAP[axis]


class Chosen:
    def __init__(self, condition, first, second):
        self.condition, self.first, self.second = condition, first, second

    def __getitem__(self, index):
        return jnp.where(self.condition, self.first[index], self.second[index])


def by_side(axis, first_ref, second_ref):
    upward = first_is_higher(axis)
    return Chosen(upward, second_ref, first_ref), Chosen(upward, first_ref, second_ref)


def row_parts(r, own_ref, below_ref, above_ref):
    if 0 <= r < H:
        wet = own_ref[2 * LEV, r : r + 1, :]
        return own_ref[0:LEV, r, :] * wet, wet, own_ref[LEV : 2 * LEV, r, :]
    ref, k = (below_ref, r + REACH) if r < 0 else (above_ref, r - H)
    field = ref[k * 8 : k * 8 + 8, :]
    m = r + H if r < 0 else r - H
    wet = ref[64 + m : 65 + m, :]
    target = None
    if -2 <= r < H + 2:
        t = r + 2 if r < 0 else r - H
        target = ref[48 + 8 * t : 56 + 8 * t, :]
    return field, wet, target


def pack_cols(own_ref, swap_one_ref, swap_two_ref, after_ref, first_ref, second_ref):
    below_ref, above_ref = by_side("gx", swap_one_ref, swap_two_ref)
    upward = first_is_higher(GY)
    lane = lax.broadcasted_iota(jnp.int32, (8, 128), 1)
    zero = jnp.zeros((8, 128), F32)
    packed = [zero] * 6
    for r in range(-REACH, H + REACH):
        field, wet, target = row_parts(r, own_ref, below_ref, above_ref)
        wet = jnp.broadcast_to(wet, (8, W))
        at, by = divmod(r + REACH, 8)
        inner = lane - 16 * by
        for side, first, moves in ((0, 0, (0, 6, 10)), (3, 128, (6, 10, 12))):
            move = [by * 16 + m for m in moves]
            v = turned(field[:, first : first + 128], move[0])
            v = jnp.where(inner < 6, v, turned(wet[:, first : first + 128], move[1]))
            if target is not None:
                v = jnp.where(inner < 10, v, turned(target[:, first : first + 128], move[2]))
            packed[side + at] = jnp.where((inner >= 0) & (inner < 12), v, packed[side + at])
    for k in range(3):
        first_ref[k * 8 : k * 8 + 8, :] = jnp.where(upward, packed[3 + k], packed[k])
        second_ref[k * 8 : k * 8 + 8, :] = jnp.where(upward, packed[k], packed[3 + k])


def row_sums(parts):
    return jnp.concatenate([jnp.sum(v * v, axis=1, keepdims=True) for v in parts], axis=0)


def prepare(
    one_ref, two_ref, head_ref, d1_ref, d2_ref, d3_ref, gid_ref,
    w1_ref, w2_ref, w3_ref, w3t_ref, w2t_ref, w1t_ref, bias_ref, choose_ref, below_ref,
):
    one, two, head = one_ref[...], two_ref[...], head_ref[...]
    w1_ref[...] = one[:, : 9 * LEV].astype(BF)
    w2_ref[...] = jnp.concatenate(
        [
            jnp.concatenate(
                [two[:, (3 * a + b) * C : (3 * a + b + 1) * C] for a in range(3)], axis=1
            )
            for b in range(3)
        ],
        axis=0,
    ).astype(BF)
    w3_ref[...] = head[:, :C].astype(BF)
    w3t_ref[...] = head[:, :C].T.astype(BF)
    w2t_ref[...] = jnp.concatenate(
        [
            jnp.concatenate(
                [two[:, (8 - 3 * a - b) * C : (9 - 3 * a - b) * C].T for a in range(3)], axis=1
            )
            for b in range(3)
        ],
        axis=0,
    ).astype(BF)
    w1t_ref[...] = jnp.concatenate(
        [
            jnp.concatenate(
                [one[:, (3 * (2 - a) + b) * LEV : (3 * (2 - a) + b + 1) * LEV].T for a in range(3)],
                axis=1,
            )
            for b in range(3)
        ],
        axis=0,
    ).astype(BF)
    bias_ref[0:64, :] = jnp.broadcast_to(one[:, 9 * LEV :], (64, 128))
    bias_ref[64:128, :] = jnp.broadcast_to(two[:, 9 * C :], (64, 128))
    bias_ref[128:160, :] = jnp.broadcast_to(head[:, C:], (32, 128))
    group = lax.broadcasted_iota(jnp.int32, (128, 160), 0)
    choose = jnp.where(gid_ref[...] == group, 1.0, 0.0).T
    choose_ref[...] = choose
    sums = jnp.sum(choose * row_sums((d1_ref[...], d2_ref[...], d3_ref[...])), axis=0, keepdims=True)
    below_ref[...] = jnp.sqrt(sums + 1e-06)


def lanes(parts):
    return parts[0] if len(parts) == 1 else jnp.concatenate(parts, axis=1)


def cut(v, n):
    return [v[:, k * PITCH : (k + 1) * PITCH] for k in range(n)]


def folded(v):
    total = v[:, :128]
    for k in range(1, v.shape[1] // 128):
        total = total + v[:, k * 128 : (k + 1) * 128]
    return total


def main(
    own_ref, row_one_ref, row_two_ref, col_one_ref, col_two_ref,
    w1_ref, w2_ref, w3_ref, w3t_ref, w2t_ref, w1t_ref, bias_ref,
    final_ref, grad_ref,
    xc0, xc1, wet_s, tgt, hm0, hm1, hc0, hc1, h2s, sp10, sp11, sp2, wd, em0, em1, e1s, rem, up, down, fin,
    b1g, b2g, b3g, g1, g2, g3, final_v, sem,
):
    below_ref, above_ref = by_side("gx", row_one_ref, row_two_ref)
    fromleft_ref, fromright_ref = by_side(GY, col_one_ref, col_two_ref)
    lane = lax.broadcasted_iota(jnp.int32, (8, 128), 1)
    zero = jnp.zeros((8, 128), F32)
    for r in range(-REACH, H + REACH):
        field, wet, target = row_parts(r, own_ref, below_ref, above_ref)
        at = (r + REACH) * 8
        block, by = divmod(r + REACH, 8)
        fl = fromleft_ref[block * 8 : block * 8 + 8, :]
        fr = fromright_ref[block * 8 : block * 8 + 8, :]

        def rim(first, width):
            right = turned(fr, -(by * 16 + first))
            left = turned(fl, -(by * 16 + first) - width)
            return jnp.where(lane < width, right, jnp.where(lane >= 128 - width, left, zero))

        row = jnp.concatenate([field, rim(0, 6)], axis=1)
        xc0[at * 3 : at * 3 + 24, :] = jnp.concatenate(
            [turned(row, 1), row, turned(row, -1)], axis=0
        )
        wet_s[at : at + 8, :] = jnp.concatenate([jnp.broadcast_to(wet, (8, W)), rim(6, 4)], axis=1)
        if target is not None:
            tgt[at : at + 8, :] = jnp.concatenate([target, rim(10, 2)], axis=1)
    for ref in (b1g, b2g, b3g, g1, g2, g3):
        ref[...] = jnp.zeros(ref.shape, F32)
    for r in (4, 5, 14, 15):
        em0[r * 64 : r * 64 + 64, :] = jnp.zeros((64, PITCH), BF)

    col = lax.broadcasted_iota(jnp.int32, (1, PITCH), 1)
    col = jnp.where(col < 320, col, col - PITCH) + lax.axis_index(GY) * W
    col_in = jnp.where((col >= 0) & (col < lax.axis_size(GY) * W), 1.0, 0.0).astype(F32)

    row0 = lax.axis_index("gx") * H

    def inside(r):
        i = row0 + r - REACH
        return col_in * jnp.where((i >= 0) & (i < lax.axis_size("gx") * H), 1.0, 0.0)

    def bias(at, n):
        b = bias_ref[at : at + n, :]
        return jnp.concatenate([b] * 3, axis=1)

    def part(ref, r, size, first=0, count=None):
        start = r * size + first
        return ref.at[start : start + (size if count is None else count), :]

    def loop(lo, hi, per, body):
        for first in range(lo, hi, per):
            body([first + REACH + k for k in range(per)])

    def thrice(v):
        return turned(v, 1), v, turned(v, -1)

    def conv(weights, ref, rs):
        y = dot(weights, lanes([part(ref, r - 1, 64, 0, 192)[...] for r in rs]))
        return [
            turned(v[0:64], 1) + v[64:128] + turned(v[128:192], -1) for v in cut(y, len(rs))
        ]

    def first_layer(xc, hm, hc, sp1):
        def body(rs):
            x9 = lanes([part(xc, r - 1, 24, 0, 72)[...].astype(BF) for r in rs])
            for r, z in zip(rs, cut(dot(w1_ref[...], x9), len(rs))):
                z = z + bias(0, 64)
                s = sigmoid(z)
                keep = inside(r)
                h = (z * s * keep).astype(BF)
                part(hm, r, 64)[...] = h
                if -1 <= r - REACH <= H:
                    for k, piece in enumerate(thrice(h)):
                        part(hc, r, 192, 64 * k, 64)[...] = piece
                    part(sp1, r, 64)[...] = silu_slope(z, s) * keep

        return body

    def second_layer(hm, rs):
        h2, slope = [], []
        for z in conv(w2_ref[...], hm, rs):
            z = z + bias(64, 64)
            s = sigmoid(z)
            h2.append((z * s).astype(BF))
            slope.append(silu_slope(z, s))
        q = cut(dot(w3_ref[...], lanes(h2)), len(rs))
        return lanes(h2), lanes(slope), lanes([sigmoid(v + bias(128, 32)) for v in q])

    def slopes(xc, r):
        x = part(xc, r, 24, 8, 8)[...]
        beside = (
            part(xc, r + 1, 24, 8, 8)[...],
            part(xc, r - 1, 24, 8, 8)[...],
            part(xc, r, 24, 16, 8)[...],
            part(xc, r, 24, 0, 8)[...],
        )
        return x, [b - x for b in beside]

    def tail_zero(rs):
        h2, slope, p = second_layer(hm0, rs)
        n = len(rs)
        for r, h2r, sr, pr in zip(rs, cut(h2, n), cut(slope, n), cut(p, n)):
            part(h2s, r, 64)[...] = h2r
            part(sp2, r, 64)[...] = sr
            x, diff = slopes(xc0, r)
            wet = part(wet_s, r, 8)[...]
            change = jnp.zeros_like(x)
            for k in range(4):
                pk = pr[8 * k : 8 * k + 8]
                move = 0.25 * pk * diff[k]
                change = change + move
                part(wd, r, 32, 8 * k, 8)[...] = wet * move * (1.0 - pk)
            for k, piece in enumerate(thrice(x + wet * change)):
                part(xc1, r, 24, 8 * k, 8)[...] = piece

    def tail_grads(rs, e3, e2, h2, hc):
        b3g[...] += sum(folded(e[:, :W]) for e in e3)
        b2g[...] += sum(folded(e[:, :W]) for e in e2)
        g3[...] += dot_nt(
            lanes([e[:, :W].astype(BF) for e in e3]), lanes([v[:, :W] for v in h2])
        )
        g2[...] += dot_nt(
            lanes([part(hc, r - 1, 192, 0, 576)[:, :W] for r in rs]),
            lanes([e[:, :W].astype(BF) for e in e2]),
        )

    def tail_one(own):
        def body(rs):
            h2, slope, p = second_layer(hm1, rs)
            n = len(rs)
            e3s = []
            for r, pr in zip(rs, cut(p, n)):
                x, diff = slopes(xc1, r)
                wet = part(wet_s, r, 8)[...]
                c = [0.25 * pr[8 * k : 8 * k + 8] for k in range(4)]
                move = [c[k] * diff[k] for k in range(4)]
                new = x + wet * (move[0] + move[1] + move[2] + move[3])
                if own:
                    part(fin, r, 8)[...] = new
                g = wet * (new - part(tgt, r, 8)[...])
                wg = wet * g
                t = [wg * c[k] for k in range(4)]
                left = g - t[0] - t[1] - t[2] - t[3]
                part(rem, r, 8)[...] = left + turned(t[2], 1) + turned(t[3], -1)
                part(up, r, 8)[...] = t[0]
                part(down, r, 8)[...] = t[1]
                e3s.append(
                    jnp.concatenate(
                        [wg * move[k] * (1.0 - pr[8 * k : 8 * k + 8]) for k in range(4)], axis=0
                    )
                )
            e2 = dot(w3t_ref[...], lanes([e.astype(BF) for e in e3s])) * slope
            e2s = cut(e2, n)
            for r, e in zip(rs, e2s):
                part(em1, r, 64)[...] = e.astype(BF)
            if own:
                tail_grads(rs, e3s, e2s, cut(h2, n), hc1)

        return body

    def first_error(em, sp1, rs):
        return [v * part(sp1, r, 64)[...] for r, v in zip(rs, conv(w2t_ref[...], em, rs))]

    def first_grads(rs, e1, xc, width):
        b1g[...] += sum(folded(e[:, :width]) for e in e1)
        g1[...] += dot_nt(
            lanes([e[:, :width].astype(BF) for e in e1]),
            lanes([part(xc, r - 1, 24, 0, 72)[:, :width].astype(BF) for r in rs]),
        )

    def first_one(own):
        def body(rs):
            e1 = first_error(em1, sp11, rs)
            for r, e in zip(rs, e1):
                part(e1s, r, 64)[...] = e.astype(BF)
            if own:
                first_grads(rs, e1, xc1, W)

        return body

    def back_zero(rs):
        y = dot(w1t_ref[...], lanes([part(e1s, r - 1, 64, 0, 192)[...] for r in rs]))
        e3s = []
        for r, yr in zip(rs, cut(y, len(rs))):
            g = part(rem, r, 8)[...] + part(up, r - 1, 8)[...] + part(down, r + 1, 8)[...]
            g = g + yr[8:16] + turned(yr[0:8], -1) + turned(yr[16:24], 1)
            e3 = jnp.concatenate([g] * 4, axis=0) * part(wd, r, 32)[...]
            e3s.append(jnp.concatenate([e3[:, :W], jnp.zeros((K, PITCH - W), F32)], axis=1))
        e2 = dot(w3t_ref[...], lanes([e.astype(BF) for e in e3s]))
        e2s = [v * part(sp2, r, 64)[...] for r, v in zip(rs, cut(e2, len(rs)))]
        for r, e in zip(rs, e2s):
            part(em0, r, 64)[...] = e.astype(BF)
        tail_grads(rs, e3s, e2s, [part(h2s, r, 64)[...] for r in rs], hc0)

    def first_zero(rs):
        first_grads(rs, first_error(em0, sp10, rs), xc0, PITCH)

    loop(-5, 13, 9, first_layer(xc0, hm0, hc0, sp10))
    loop(-4, 12, 16, tail_zero)
    loop(-3, 11, 14, first_layer(xc1, hm1, hc1, sp11))
    tail_one(False)([4, 5, 14, 15])
    loop(0, 8, 8, tail_one(True))
    for r in range(H):
        final_v[:, r, :] = fin[(r + REACH) * 8 : (r + REACH) * 8 + 8, :W]
    out = pltpu.make_async_copy(final_v, final_ref, sem)
    out.start()
    first_one(False)([5, 14])
    loop(0, 8, 8, first_one(True))
    loop(0, 8, 8, back_zero)
    loop(-1, 9, 10, first_zero)

    grad_ref[0:256, :] = jnp.concatenate([g2[0:256, :], g2[256:512, :]], axis=1)
    grad_ref[256:320, :] = jnp.concatenate([g2[512:576, :], g1[:, 0:64]], axis=1)
    sums = [jnp.sum(ref[...], axis=1, keepdims=True) for ref in (b1g, b2g, b3g)]
    sums[2] = jnp.concatenate([sums[2], jnp.zeros((32, 1), F32)], axis=0)
    grad_ref[320:384, :] = jnp.concatenate(
        [
            g1[:, 64:72],
            *sums,
            jnp.zeros((64, 53), F32),
            jnp.concatenate([g3[...], jnp.zeros((32, 64), F32)], axis=0),
        ],
        axis=1,
    )
    out.wait()


def finish(total_ref, d1_ref, d2_ref, d3_ref, choose_ref, below_ref, u1_ref, u2_ref, u3_ref):
    t = [total_ref[k * 64 : k * 64 + 64, :] for k in range(6)]
    two = jnp.concatenate([v[:, :64].T for v in t[:4]] + [v[:, 64:].T for v in t[:4]] + [t[4][:, :64].T, t[5][:, 9:10]], axis=1)
    one = jnp.concatenate([t[4][:, 64:], t[5][:, :8], t[5][:, 8:9]], axis=1)
    three = jnp.concatenate([t[5][:32, 64:], t[5][:32, 10:11]], axis=1)
    grads = (one, two, three)
    squares = row_sums(grads)
    norm = jnp.sqrt(jnp.sum(squares, axis=0, keepdims=True))
    factor = 1.0 / jnp.maximum(norm, 1.0)
    clipped = [v * factor for v in grads]
    choose = choose_ref[...]
    ratios = factor * jnp.sqrt(jnp.sum(choose * squares, axis=0, keepdims=True)) / below_ref[...]
    row_ratio = jnp.sum(choose * ratios, axis=1, keepdims=True)
    scaling = math.sqrt(PARAMS)
    at = 0
    for ref, v, d_ref in zip((u1_ref, u2_ref, u3_ref), clipped, (d1_ref, d2_ref, d3_ref)):
        n = v.shape[0]
        ref[...] = scaling * (v + row_ratio[at : at + n] * d_ref[...])
        at += n


def shape(dims, dtype=F32):
    return jax.ShapeDtypeStruct(dims, dtype)


def kernel(body, outs, cost, mib, **more):
    return pl.pallas_call(
        body,
        out_shape=outs,
        cost_estimate=pl.CostEstimate(flops=cost, bytes_accessed=cost, transcendentals=0),
        compiler_params=pltpu.CompilerParams(vmem_limit_bytes=mib * 2**20),
        **more,
    )


def exchange(first, second, axis):
    count = lax.axis_size(axis)
    starts = (FIRST_SWAP[axis], 1 - FIRST_SWAP[axis])
    pairs = [[(i, i + 1) for i in range(start, count - 1, 2)] for start in starts]
    swaps = [[*p, *((b, a) for a, b in p)] for p in pairs]
    return lax.ppermute(first, axis, swaps[0]), lax.ppermute(second, axis, swaps[1])


def total_of(grad):
    near = ("gy_0", "gy_1")
    n = lax.axis_size(near)
    pieces = grad.reshape(n, -1, 128)
    own = jnp.sum(lax.all_to_all(pieces, near, 0, 0, tiled=True), axis=0)
    own = own + lax.ppermute(own, "gy_2", [(0, 1), (1, 0)])
    m = lax.axis_size("gx")
    copies = jnp.broadcast_to(own, (m, *own.shape))
    own = jnp.sum(lax.all_to_all(copies, "gx", 0, 0, tiled=True), axis=0)
    copies = jnp.broadcast_to(own, (n, *own.shape))
    return lax.all_to_all(copies, near, 0, 0, tiled=True).reshape(grad.shape)


def per_device(init, target, mask, one, two, head, d1, d2, d3, gid):
    hbm = pl.BlockSpec(memory_space=pltpu.HBM)
    vmem = pl.BlockSpec(memory_space=pltpu.VMEM)
    def widened(v, first):
        return jnp.pad(v, ((first, 2 * LEV + 1 - first - v.shape[0]), (0, 0), (0, 0)))

    own = widened(init, 0) + widened(target, LEV) + widened(mask[None], 2 * LEV).astype(F32)
    packs = kernel(pack_rows, [shape((72, W))] * 2, 10**5, 4)(own)
    rows_in = exchange(*packs, "gx")
    *weights, choose, below_ratio = kernel(
        prepare,
        [
            shape((C, 72), BF), shape((192, 192), BF), shape((K, C), BF), shape((C, K), BF),
            shape((192, 192), BF), shape((24, 192), BF), shape((160, 128)),
            shape((160, 128)), shape((1, 128)),
        ],
        10**6,
        8,
    )(one, two, head, d1, d2, d3, gid.reshape(1, -1))
    packs = kernel(pack_cols, [shape((24, 128))] * 2, 10**5, 4)(
        own, *rows_in, weights[6]
    )
    cols_in = exchange(*packs, GY)

    def rows(size, dtype=F32):
        return pltpu.VMEM((20 * size, PITCH), dtype)

    final, grad = kernel(
        main,
        [shape((LEV, H, W)), shape((384, 128))],
        10**7,
        40,
        in_specs=[vmem] * 12,
        out_specs=[hbm, vmem],
        scratch_shapes=[
            rows(24), rows(24), rows(8), rows(8), rows(64, BF), rows(64, BF), rows(192, BF), rows(192, BF), rows(64, BF),
            rows(64), rows(64), rows(64), rows(32), rows(64, BF), rows(64, BF), rows(64, BF),
            rows(8), rows(8), rows(8), rows(8),
            pltpu.VMEM((64, 128), F32), pltpu.VMEM((64, 128), F32), pltpu.VMEM((32, 128), F32),
            pltpu.VMEM((64, 72), F32), pltpu.VMEM((576, 64), F32), pltpu.VMEM((32, 64), F32),
            pltpu.VMEM((LEV, H, W), F32), pltpu.SemaphoreType.DMA,
        ],
    )(own, *rows_in, *cols_in, *weights)
    total = total_of(grad)
    u1, u2, u3 = kernel(finish, [shape(one.shape), shape(two.shape), shape(head.shape)], 10**6, 8)(
        total, d1, d2, d3, choose, below_ratio
    )
    return final, u1, u2, u3


def solution(mesh):
    count = mesh.shape["gy"] // 8
    torus = Mesh(mesh.devices.reshape(mesh.shape["gx"], count, 4, 2), ("gx", *GY))
    placed = (P(None, "gx", GY), P(None, "gx", GY), P("gx", GY), P(), P(), P(), P(), P(), P(), P())
    return jax.shard_map(
        per_device,
        mesh=torus,
        in_specs=placed,
        out_specs=(P(None, "gx", GY), P(), P(), P()),
        check_vma=False,
    )
```

```python
import math

import jax
import jax.numpy as jnp
from jax import lax
from jax.experimental import pallas as pl
from jax.experimental.pallas import tpu as pltpu
from jax.sharding import Mesh
from jax.sharding import PartitionSpec as P

LEV = 8
C = 64
K = 32
GROUPS = 6
PARAMS = 43680
GY = ("gy_0", "gy_1", "gy_2")
H = 8
W = 256
PITCH = 384
REACH = 6
BF = jnp.bfloat16
F32 = jnp.float32
NT = (((1,), (1,)), ((), ()))


def dot(a, b):
    return jnp.dot(a, b, preferred_element_type=F32)


def dot_nt(a, b):
    return lax.dot_general(a, b, NT, preferred_element_type=F32)


def turned(v, by):
    return pltpu.roll(v, by % v.shape[1], 1)


def sigmoid(v):
    return 0.5 * jnp.tanh(0.5 * v) + 0.5


def silu_slope(v, s):
    return s * (1.0 + v * (1.0 - s))


def pack_rows(own_ref, first_ref, second_ref):
    upward = first_is_higher("gx")
    wet = own_ref[2 * LEV, :, :]

    def put(at, low, high):
        first_ref[at : at + 8, :] = jnp.where(upward, high, low)
        second_ref[at : at + 8, :] = jnp.where(upward, low, high)

    put(64, wet, wet)
    for k in range(REACH):
        r = H - REACH + k
        put(k * 8, own_ref[0:LEV, k, :] * wet[k : k + 1], own_ref[0:LEV, r, :] * wet[r : r + 1])
    for k in range(2):
        put(48 + k * 8, own_ref[LEV : 2 * LEV, k, :], own_ref[LEV : 2 * LEV, H - 2 + k, :])


FIRST_SWAP = {"gx": 0, GY: 1}


def first_is_higher(axis):
    return lax.rem(lax.axis_index(axis), 2) == FIRST_SWAP[axis]


class Chosen:
    def __init__(self, condition, first, second):
        self.condition, self.first, self.second = condition, first, second

    def __getitem__(self, index):
        return jnp.where(self.condition, self.first[index], self.second[index])


def by_side(axis, first_ref, second_ref):
    upward = first_is_higher(axis)
    return Chosen(upward, second_ref, first_ref), Chosen(upward, first_ref, second_ref)


def row_parts(r, own_ref, below_ref, above_ref):
    if 0 <= r < H:
        wet = own_ref[2 * LEV, r : r + 1, :]
        return own_ref[0:LEV, r, :] * wet, wet, own_ref[LEV : 2 * LEV, r, :]
    ref, k = (below_ref, r + REACH) if r < 0 else (above_ref, r - H)
    field = ref[k * 8 : k * 8 + 8, :]
    m = r + H if r < 0 else r - H
    wet = ref[64 + m : 65 + m, :]
    target = None
    if -2 <= r < H + 2:
        t = r + 2 if r < 0 else r - H
        target = ref[48 + 8 * t : 56 + 8 * t, :]
    return field, wet, target


def pack_cols(own_ref, swap_one_ref, swap_two_ref, after_ref, first_ref, second_ref):
    below_ref, above_ref = by_side("gx", swap_one_ref, swap_two_ref)
    upward = first_is_higher(GY)
    lane = lax.broadcasted_iota(jnp.int32, (8, 128), 1)
    zero = jnp.zeros((8, 128), F32)
    packed = [zero] * 6
    for r in range(-REACH, H + REACH):
        field, wet, target = row_parts(r, own_ref, below_ref, above_ref)
        wet = jnp.broadcast_to(wet, (8, W))
        at, by = divmod(r + REACH, 8)
        inner = lane - 16 * by
        for side, first, moves in ((0, 0, (0, 6, 10)), (3, 128, (6, 10, 12))):
            move = [by * 16 + m for m in moves]
            v = turned(field[:, first : first + 128], move[0])
            v = jnp.where(inner < 6, v, turned(wet[:, first : first + 128], move[1]))
            if target is not None:
                v = jnp.where(inner < 10, v, turned(target[:, first : first + 128], move[2]))
            packed[side + at] = jnp.where((inner >= 0) & (inner < 12), v, packed[side + at])
    for k in range(3):
        first_ref[k * 8 : k * 8 + 8, :] = jnp.where(upward, packed[3 + k], packed[k])
        second_ref[k * 8 : k * 8 + 8, :] = jnp.where(upward, packed[k], packed[3 + k])


def row_sums(parts):
    return jnp.concatenate([jnp.sum(v * v, axis=1, keepdims=True) for v in parts], axis=0)


def prepare(
    one_ref, two_ref, head_ref, d1_ref, d2_ref, d3_ref, gid_ref,
    w1_ref, w2_ref, w3_ref, w3t_ref, w2t_ref, w1t_ref, bias_ref, choose_ref, below_ref,
):
    one, two, head = one_ref[...], two_ref[...], head_ref[...]
    w1_ref[...] = one[:, : 9 * LEV].astype(BF)
    w2_ref[...] = jnp.concatenate(
        [
            jnp.concatenate(
                [two[:, (3 * a + b) * C : (3 * a + b + 1) * C] for a in range(3)], axis=1
            )
            for b in range(3)
        ],
        axis=0,
    ).astype(BF)
    w3_ref[...] = head[:, :C].astype(BF)
    w3t_ref[...] = head[:, :C].T.astype(BF)
    w2t_ref[...] = jnp.concatenate(
        [
            jnp.concatenate(
                [two[:, (8 - 3 * a - b) * C : (9 - 3 * a - b) * C].T for a in range(3)], axis=1
            )
            for b in range(3)
        ],
        axis=0,
    ).astype(BF)
    w1t_ref[...] = jnp.concatenate(
        [
            jnp.concatenate(
                [one[:, (3 * (2 - a) + b) * LEV : (3 * (2 - a) + b + 1) * LEV].T for a in range(3)],
                axis=1,
            )
            for b in range(3)
        ],
        axis=0,
    ).astype(BF)
    bias_ref[0:64, :] = jnp.broadcast_to(one[:, 9 * LEV :], (64, 128))
    bias_ref[64:128, :] = jnp.broadcast_to(two[:, 9 * C :], (64, 128))
    bias_ref[128:160, :] = jnp.broadcast_to(head[:, C:], (32, 128))
    group = lax.broadcasted_iota(jnp.int32, (128, 160), 0)
    choose = jnp.where(gid_ref[...] == group, 1.0, 0.0).T
    choose_ref[...] = choose
    sums = jnp.sum(choose * row_sums((d1_ref[...], d2_ref[...], d3_ref[...])), axis=0, keepdims=True)
    below_ref[...] = jnp.sqrt(sums + 1e-06)


def lanes(parts):
    return parts[0] if len(parts) == 1 else jnp.concatenate(parts, axis=1)


def cut(v, n):
    return [v[:, k * PITCH : (k + 1) * PITCH] for k in range(n)]


def folded(v):
    total = v[:, :128]
    for k in range(1, v.shape[1] // 128):
        total = total + v[:, k * 128 : (k + 1) * 128]
    return total


def main(
    own_ref, row_one_ref, row_two_ref, col_one_ref, col_two_ref,
    w1_ref, w2_ref, w3_ref, w3t_ref, w2t_ref, w1t_ref, bias_ref,
    final_ref, grad_ref,
    xc0, xc1, wet_s, tgt, hm0, hm1, hc0, hc1, h2s, sp10, sp11, sp2, wd, em0, em1, e1s, rem, up, down, fin,
    b1g, b2g, b3g, g1, g2, g3, final_v, sem,
):
    below_ref, above_ref = by_side("gx", row_one_ref, row_two_ref)
    fromleft_ref, fromright_ref = by_side(GY, col_one_ref, col_two_ref)
    lane = lax.broadcasted_iota(jnp.int32, (8, 128), 1)
    zero = jnp.zeros((8, 128), F32)
    for r in range(-REACH, H + REACH):
        field, wet, target = row_parts(r, own_ref, below_ref, above_ref)
        at = (r + REACH) * 8
        block, by = divmod(r + REACH, 8)
        fl = fromleft_ref[block * 8 : block * 8 + 8, :]
        fr = fromright_ref[block * 8 : block * 8 + 8, :]

        def rim(first, width):
            right = turned(fr, -(by * 16 + first))
            left = turned(fl, -(by * 16 + first) - width)
            return jnp.where(lane < width, right, jnp.where(lane >= 128 - width, left, zero))

        row = jnp.concatenate([field, rim(0, 6)], axis=1)
        xc0[at * 3 : at * 3 + 24, :] = jnp.concatenate(
            [turned(row, 1), row, turned(row, -1)], axis=0
        )
        wet_s[at : at + 8, :] = jnp.concatenate([jnp.broadcast_to(wet, (8, W)), rim(6, 4)], axis=1)
        if target is not None:
            tgt[at : at + 8, :] = jnp.concatenate([target, rim(10, 2)], axis=1)
    for ref in (b1g, b2g, b3g, g1, g2, g3):
        ref[...] = jnp.zeros(ref.shape, F32)
    for r in (4, 5, 14, 15):
        em0[r * 64 : r * 64 + 64, :] = jnp.zeros((64, PITCH), BF)

    col = lax.broadcasted_iota(jnp.int32, (1, PITCH), 1)
    col = jnp.where(col < 320, col, col - PITCH) + lax.axis_index(GY) * W
    col_in = jnp.where((col >= 0) & (col < lax.axis_size(GY) * W), 1.0, 0.0).astype(F32)

    row0 = lax.axis_index("gx") * H

    def inside(r):
        i = row0 + r - REACH
        return col_in * jnp.where((i >= 0) & (i < lax.axis_size("gx") * H), 1.0, 0.0)

    def bias(at, n):
        b = bias_ref[at : at + n, :]
        return jnp.concatenate([b] * 3, axis=1)

    def part(ref, r, size, first=0, count=None):
        start = r * size + first
        return ref.at[start : start + (size if count is None else count), :]

    def loop(lo, hi, per, body):
        for first in range(lo, hi, per):
            body([first + REACH + k for k in range(per)])

    def thrice(v):
        return turned(v, 1), v, turned(v, -1)

    def conv(weights, ref, rs):
        y = dot(weights, lanes([part(ref, r - 1, 64, 0, 192)[...] for r in rs]))
        return [
            turned(v[0:64], 1) + v[64:128] + turned(v[128:192], -1) for v in cut(y, len(rs))
        ]

    def first_layer(xc, hm, hc, sp1):
        def body(rs):
            x9 = lanes([part(xc, r - 1, 24, 0, 72)[...].astype(BF) for r in rs])
            for r, z in zip(rs, cut(dot(w1_ref[...], x9), len(rs))):
                z = z + bias(0, 64)
                s = sigmoid(z)
                keep = inside(r)
                h = (z * s * keep).astype(BF)
                part(hm, r, 64)[...] = h
                if -1 <= r - REACH <= H:
                    for k, piece in enumerate(thrice(h)):
                        part(hc, r, 192, 64 * k, 64)[...] = piece
                    part(sp1, r, 64)[...] = silu_slope(z, s) * keep

        return body

    def second_layer(hm, rs):
        h2, slope = [], []
        for z in conv(w2_ref[...], hm, rs):
            z = z + bias(64, 64)
            s = sigmoid(z)
            h2.append((z * s).astype(BF))
            slope.append(silu_slope(z, s))
        q = cut(dot(w3_ref[...], lanes(h2)), len(rs))
        return lanes(h2), lanes(slope), lanes([sigmoid(v + bias(128, 32)) for v in q])

    def slopes(xc, r):
        x = part(xc, r, 24, 8, 8)[...]
        beside = (
            part(xc, r + 1, 24, 8, 8)[...],
            part(xc, r - 1, 24, 8, 8)[...],
            part(xc, r, 24, 16, 8)[...],
            part(xc, r, 24, 0, 8)[...],
        )
        return x, [b - x for b in beside]

    def tail_zero(rs):
        h2, slope, p = second_layer(hm0, rs)
        n = len(rs)
        for r, h2r, sr, pr in zip(rs, cut(h2, n), cut(slope, n), cut(p, n)):
            part(h2s, r, 64)[...] = h2r
            part(sp2, r, 64)[...] = sr
            x, diff = slopes(xc0, r)
            wet = part(wet_s, r, 8)[...]
            change = jnp.zeros_like(x)
            for k in range(4):
                pk = pr[8 * k : 8 * k + 8]
                move = 0.25 * pk * diff[k]
                change = change + move
                part(wd, r, 32, 8 * k, 8)[...] = wet * move * (1.0 - pk)
            for k, piece in enumerate(thrice(x + wet * change)):
                part(xc1, r, 24, 8 * k, 8)[...] = piece

    def tail_grads(rs, e3, e2, h2, hc):
        b3g[...] += sum(folded(e[:, :W]) for e in e3)
        b2g[...] += sum(folded(e[:, :W]) for e in e2)
        g3[...] += dot_nt(
            lanes([e[:, :W].astype(BF) for e in e3]), lanes([v[:, :W] for v in h2])
        )
        g2[...] += dot_nt(
            lanes([part(hc, r - 1, 192, 0, 576)[:, :W] for r in rs]),
            lanes([e[:, :W].astype(BF) for e in e2]),
        )

    def of_block(rs, arrays):
        return [v for r, v in zip(rs, arrays) if 0 <= r - REACH < H]

    def tail_one(rs):
        h2, slope, p = second_layer(hm1, rs)
        n = len(rs)
        e3s = []
        for r, pr in zip(rs, cut(p, n)):
            x, diff = slopes(xc1, r)
            wet = part(wet_s, r, 8)[...]
            c = [0.25 * pr[8 * k : 8 * k + 8] for k in range(4)]
            move = [c[k] * diff[k] for k in range(4)]
            new = x + wet * (move[0] + move[1] + move[2] + move[3])
            if 0 <= r - REACH < H:
                part(fin, r, 8)[...] = new
            g = wet * (new - part(tgt, r, 8)[...])
            wg = wet * g
            t = [wg * c[k] for k in range(4)]
            left = g - t[0] - t[1] - t[2] - t[3]
            part(rem, r, 8)[...] = left + turned(t[2], 1) + turned(t[3], -1)
            part(up, r, 8)[...] = t[0]
            part(down, r, 8)[...] = t[1]
            e3s.append(
                jnp.concatenate(
                    [wg * move[k] * (1.0 - pr[8 * k : 8 * k + 8]) for k in range(4)], axis=0
                )
            )
        e2 = dot(w3t_ref[...], lanes([e.astype(BF) for e in e3s])) * slope
        e2s = cut(e2, n)
        for r, e in zip(rs, e2s):
            part(em1, r, 64)[...] = e.astype(BF)
        tail_grads(of_block(rs, rs), of_block(rs, e3s), of_block(rs, e2s), of_block(rs, cut(h2, n)), hc1)

    def first_error(em, sp1, rs):
        return [v * part(sp1, r, 64)[...] for r, v in zip(rs, conv(w2t_ref[...], em, rs))]

    def first_grads(rs, e1, xc, width):
        b1g[...] += sum(folded(e[:, :width]) for e in e1)
        g1[...] += dot_nt(
            lanes([e[:, :width].astype(BF) for e in e1]),
            lanes([part(xc, r - 1, 24, 0, 72)[:, :width].astype(BF) for r in rs]),
        )

    def first_one(rs):
        e1 = first_error(em1, sp11, rs)
        for r, e in zip(rs, e1):
            part(e1s, r, 64)[...] = e.astype(BF)
        first_grads(of_block(rs, rs), of_block(rs, e1), xc1, W)

    def back_zero(rs):
        y = dot(w1t_ref[...], lanes([part(e1s, r - 1, 64, 0, 192)[...] for r in rs]))
        e3s = []
        for r, yr in zip(rs, cut(y, len(rs))):
            g = part(rem, r, 8)[...] + part(up, r - 1, 8)[...] + part(down, r + 1, 8)[...]
            g = g + yr[8:16] + turned(yr[0:8], -1) + turned(yr[16:24], 1)
            e3 = jnp.concatenate([g] * 4, axis=0) * part(wd, r, 32)[...]
            e3s.append(jnp.concatenate([e3[:, :W], jnp.zeros((K, PITCH - W), F32)], axis=1))
        e2 = dot(w3t_ref[...], lanes([e.astype(BF) for e in e3s]))
        e2s = [v * part(sp2, r, 64)[...] for r, v in zip(rs, cut(e2, len(rs)))]
        for r, e in zip(rs, e2s):
            part(em0, r, 64)[...] = e.astype(BF)
        tail_grads(rs, e3s, e2s, [part(h2s, r, 64)[...] for r in rs], hc0)

    def first_zero(rs):
        first_grads(rs, first_error(em0, sp10, rs), xc0, PITCH)

    loop(-5, 13, 9, first_layer(xc0, hm0, hc0, sp10))
    loop(-4, 12, 16, tail_zero)
    loop(-3, 11, 14, first_layer(xc1, hm1, hc1, sp11))
    loop(-2, 10, 12, tail_one)
    for r in range(H):
        final_v[:, r, :] = fin[(r + REACH) * 8 : (r + REACH) * 8 + 8, :W]
    out = pltpu.make_async_copy(final_v, final_ref, sem)
    out.start()
    loop(-1, 9, 10, first_one)
    loop(0, 8, 8, back_zero)
    loop(-1, 9, 10, first_zero)

    grad_ref[0:256, :] = jnp.concatenate([g2[0:256, :], g2[256:512, :]], axis=1)
    grad_ref[256:320, :] = jnp.concatenate([g2[512:576, :], g1[:, 0:64]], axis=1)
    sums = [jnp.sum(ref[...], axis=1, keepdims=True) for ref in (b1g, b2g, b3g)]
    sums[2] = jnp.concatenate([sums[2], jnp.zeros((32, 1), F32)], axis=0)
    grad_ref[320:384, :] = jnp.concatenate(
        [
            g1[:, 64:72],
            *sums,
            jnp.zeros((64, 53), F32),
            jnp.concatenate([g3[...], jnp.zeros((32, 64), F32)], axis=0),
        ],
        axis=1,
    )
    out.wait()


def finish(total_ref, d1_ref, d2_ref, d3_ref, choose_ref, below_ref, u1_ref, u2_ref, u3_ref):
    t = [total_ref[k * 64 : k * 64 + 64, :] for k in range(6)]
    two = jnp.concatenate([v[:, :64].T for v in t[:4]] + [v[:, 64:].T for v in t[:4]] + [t[4][:, :64].T, t[5][:, 9:10]], axis=1)
    one = jnp.concatenate([t[4][:, 64:], t[5][:, :8], t[5][:, 8:9]], axis=1)
    three = jnp.concatenate([t[5][:32, 64:], t[5][:32, 10:11]], axis=1)
    grads = (one, two, three)
    squares = row_sums(grads)
    norm = jnp.sqrt(jnp.sum(squares, axis=0, keepdims=True))
    factor = 1.0 / jnp.maximum(norm, 1.0)
    clipped = [v * factor for v in grads]
    choose = choose_ref[...]
    ratios = factor * jnp.sqrt(jnp.sum(choose * squares, axis=0, keepdims=True)) / below_ref[...]
    row_ratio = jnp.sum(choose * ratios, axis=1, keepdims=True)
    scaling = math.sqrt(PARAMS)
    at = 0
    for ref, v, d_ref in zip((u1_ref, u2_ref, u3_ref), clipped, (d1_ref, d2_ref, d3_ref)):
        n = v.shape[0]
        ref[...] = scaling * (v + row_ratio[at : at + n] * d_ref[...])
        at += n


def shape(dims, dtype=F32):
    return jax.ShapeDtypeStruct(dims, dtype)


def kernel(body, outs, cost, mib, **more):
    return pl.pallas_call(
        body,
        out_shape=outs,
        cost_estimate=pl.CostEstimate(flops=cost, bytes_accessed=cost, transcendentals=0),
        compiler_params=pltpu.CompilerParams(vmem_limit_bytes=mib * 2**20),
        **more,
    )


def exchange(first, second, axis):
    count = lax.axis_size(axis)
    starts = (FIRST_SWAP[axis], 1 - FIRST_SWAP[axis])
    pairs = [[(i, i + 1) for i in range(start, count - 1, 2)] for start in starts]
    swaps = [[*p, *((b, a) for a, b in p)] for p in pairs]
    return lax.ppermute(first, axis, swaps[0]), lax.ppermute(second, axis, swaps[1])


def total_of(grad):
    near = ("gy_0", "gy_1")
    n = lax.axis_size(near)
    pieces = grad.reshape(n, -1, 128)
    own = jnp.sum(lax.all_to_all(pieces, near, 0, 0, tiled=True), axis=0)
    own = own + lax.ppermute(own, "gy_2", [(0, 1), (1, 0)])
    m = lax.axis_size("gx")
    copies = jnp.broadcast_to(own, (m, *own.shape))
    own = jnp.sum(lax.all_to_all(copies, "gx", 0, 0, tiled=True), axis=0)
    copies = jnp.broadcast_to(own, (n, *own.shape))
    return lax.all_to_all(copies, near, 0, 0, tiled=True).reshape(grad.shape)


def per_device(init, target, mask, one, two, head, d1, d2, d3, gid):
    hbm = pl.BlockSpec(memory_space=pltpu.HBM)
    vmem = pl.BlockSpec(memory_space=pltpu.VMEM)
    def widened(v, first):
        return jnp.pad(v, ((first, 2 * LEV + 1 - first - v.shape[0]), (0, 0), (0, 0)))

    own = widened(init, 0) + widened(target, LEV) + widened(mask[None], 2 * LEV).astype(F32)
    packs = kernel(pack_rows, [shape((72, W))] * 2, 10**5, 4)(own)
    rows_in = exchange(*packs, "gx")
    *weights, choose, below_ratio = kernel(
        prepare,
        [
            shape((C, 72), BF), shape((192, 192), BF), shape((K, C), BF), shape((C, K), BF),
            shape((192, 192), BF), shape((24, 192), BF), shape((160, 128)),
            shape((160, 128)), shape((1, 128)),
        ],
        10**6,
        8,
    )(one, two, head, d1, d2, d3, gid.reshape(1, -1))
    packs = kernel(pack_cols, [shape((24, 128))] * 2, 10**5, 4)(
        own, *rows_in, weights[6]
    )
    cols_in = exchange(*packs, GY)

    def rows(size, dtype=F32):
        return pltpu.VMEM((20 * size, PITCH), dtype)

    final, grad = kernel(
        main,
        [shape((LEV, H, W)), shape((384, 128))],
        10**7,
        40,
        in_specs=[vmem] * 12,
        out_specs=[hbm, vmem],
        scratch_shapes=[
            rows(24), rows(24), rows(8), rows(8), rows(64, BF), rows(64, BF), rows(192, BF), rows(192, BF), rows(64, BF),
            rows(64), rows(64), rows(64), rows(32), rows(64, BF), rows(64, BF), rows(64, BF),
            rows(8), rows(8), rows(8), rows(8),
            pltpu.VMEM((64, 128), F32), pltpu.VMEM((64, 128), F32), pltpu.VMEM((32, 128), F32),
            pltpu.VMEM((64, 72), F32), pltpu.VMEM((576, 64), F32), pltpu.VMEM((32, 64), F32),
            pltpu.VMEM((LEV, H, W), F32), pltpu.SemaphoreType.DMA,
        ],
    )(own, *rows_in, *cols_in, *weights)
    total = total_of(grad)
    u1, u2, u3 = kernel(finish, [shape(one.shape), shape(two.shape), shape(head.shape)], 10**6, 8)(
        total, d1, d2, d3, choose, below_ratio
    )
    return final, u1, u2, u3


def solution(mesh):
    count = mesh.shape["gy"] // 8
    torus = Mesh(mesh.devices.reshape(mesh.shape["gx"], count, 4, 2), ("gx", *GY))
    placed = (P(None, "gx", GY), P(None, "gx", GY), P("gx", GY), P(), P(), P(), P(), P(), P(), P())
    return jax.shard_map(
        per_device,
        mesh=torus,
        in_specs=placed,
        out_specs=(P(None, "gx", GY), P(), P(), P()),
        check_vma=False,
    )
```

```python
import math

import jax
import jax.numpy as jnp
from jax import lax
from jax.experimental import pallas as pl
from jax.experimental.pallas import tpu as pltpu
from jax.sharding import Mesh
from jax.sharding import PartitionSpec as P

LEV = 8
C = 64
K = 32
GROUPS = 6
PARAMS = 43680
GY = ("gy_0", "gy_1", "gy_2")
H = 8
W = 256
PITCH = 384
REACH = 6
BF = jnp.bfloat16
F32 = jnp.float32
NT = (((1,), (1,)), ((), ()))


def dot(a, b):
    return jnp.dot(a, b, preferred_element_type=F32)


def dot_nt(a, b):
    return lax.dot_general(a, b, NT, preferred_element_type=F32)


def turned(v, by):
    return pltpu.roll(v, by % v.shape[1], 1)


def sigmoid(v):
    return 0.5 * jnp.tanh(0.5 * v) + 0.5


def silu_slope(v, s):
    return s * (1.0 + v * (1.0 - s))


def pack_rows(own_ref, first_ref, second_ref):
    upward = first_is_higher("gx")
    wet = own_ref[2 * LEV, :, :]

    def put(at, low, high):
        first_ref[at : at + 8, :] = jnp.where(upward, high, low)
        second_ref[at : at + 8, :] = jnp.where(upward, low, high)

    put(64, wet, wet)
    for k in range(REACH):
        r = H - REACH + k
        put(k * 8, own_ref[0:LEV, k, :] * wet[k : k + 1], own_ref[0:LEV, r, :] * wet[r : r + 1])
    for k in range(2):
        put(48 + k * 8, own_ref[LEV : 2 * LEV, k, :], own_ref[LEV : 2 * LEV, H - 2 + k, :])


FIRST_SWAP = {"gx": 0, GY: 1}


def first_is_higher(axis):
    return lax.rem(lax.axis_index(axis), 2) == FIRST_SWAP[axis]


class Chosen:
    def __init__(self, condition, first, second):
        self.condition, self.first, self.second = condition, first, second

    def __getitem__(self, index):
        return jnp.where(self.condition, self.first[index], self.second[index])


def by_side(axis, first_ref, second_ref):
    upward = first_is_higher(axis)
    return Chosen(upward, second_ref, first_ref), Chosen(upward, first_ref, second_ref)


def row_parts(r, own_ref, below_ref, above_ref):
    if 0 <= r < H:
        wet = own_ref[2 * LEV, r : r + 1, :]
        return own_ref[0:LEV, r, :] * wet, wet, own_ref[LEV : 2 * LEV, r, :]
    ref, k = (below_ref, r + REACH) if r < 0 else (above_ref, r - H)
    field = ref[k * 8 : k * 8 + 8, :]
    m = r + H if r < 0 else r - H
    wet = ref[64 + m : 65 + m, :]
    target = None
    if -2 <= r < H + 2:
        t = r + 2 if r < 0 else r - H
        target = ref[48 + 8 * t : 56 + 8 * t, :]
    return field, wet, target


def pack_cols(own_ref, swap_one_ref, swap_two_ref, after_ref, first_ref, second_ref):
    below_ref, above_ref = by_side("gx", swap_one_ref, swap_two_ref)
    upward = first_is_higher(GY)
    lane = lax.broadcasted_iota(jnp.int32, (8, 128), 1)
    zero = jnp.zeros((8, 128), F32)
    packed = [zero] * 6
    for r in range(-REACH, H + REACH):
        field, wet, target = row_parts(r, own_ref, below_ref, above_ref)
        wet = jnp.broadcast_to(wet, (8, W))
        at, by = divmod(r + REACH, 8)
        inner = lane - 16 * by
        for side, first, moves in ((0, 0, (0, 6, 10)), (3, 128, (6, 10, 12))):
            move = [by * 16 + m for m in moves]
            v = turned(field[:, first : first + 128], move[0])
            v = jnp.where(inner < 6, v, turned(wet[:, first : first + 128], move[1]))
            if target is not None:
                v = jnp.where(inner < 10, v, turned(target[:, first : first + 128], move[2]))
            packed[side + at] = jnp.where((inner >= 0) & (inner < 12), v, packed[side + at])
    for k in range(3):
        first_ref[k * 8 : k * 8 + 8, :] = jnp.where(upward, packed[3 + k], packed[k])
        second_ref[k * 8 : k * 8 + 8, :] = jnp.where(upward, packed[k], packed[3 + k])


def row_sums(parts):
    return jnp.concatenate([jnp.sum(v * v, axis=1, keepdims=True) for v in parts], axis=0)


def prepare(
    one_ref, two_ref, head_ref, d1_ref, d2_ref, d3_ref, gid_ref,
    w1_ref, w2_ref, w3_ref, w3t_ref, w2t_ref, w1t_ref, bias_ref, choose_ref, below_ref,
):
    one, two, head = one_ref[...], two_ref[...], head_ref[...]
    w1_ref[...] = one[:, : 9 * LEV].astype(BF)
    w2_ref[...] = jnp.concatenate(
        [
            jnp.concatenate(
                [two[:, (3 * a + b) * C : (3 * a + b + 1) * C] for a in range(3)], axis=1
            )
            for b in range(3)
        ],
        axis=0,
    ).astype(BF)
    w3_ref[...] = head[:, :C].astype(BF)
    w3t_ref[...] = head[:, :C].T.astype(BF)
    w2t_ref[...] = jnp.concatenate(
        [
            jnp.concatenate(
                [two[:, (8 - 3 * a - b) * C : (9 - 3 * a - b) * C].T for a in range(3)], axis=1
            )
            for b in range(3)
        ],
        axis=0,
    ).astype(BF)
    w1t_ref[...] = jnp.concatenate(
        [
            jnp.concatenate(
                [one[:, (3 * (2 - a) + b) * LEV : (3 * (2 - a) + b + 1) * LEV].T for a in range(3)],
                axis=1,
            )
            for b in range(3)
        ],
        axis=0,
    ).astype(BF)
    bias_ref[0:64, :] = jnp.broadcast_to(one[:, 9 * LEV :], (64, 128))
    bias_ref[64:128, :] = jnp.broadcast_to(two[:, 9 * C :], (64, 128))
    bias_ref[128:160, :] = jnp.broadcast_to(head[:, C:], (32, 128))
    group = lax.broadcasted_iota(jnp.int32, (128, 160), 0)
    choose = jnp.where(gid_ref[...] == group, 1.0, 0.0).T
    choose_ref[...] = choose
    sums = jnp.sum(choose * row_sums((d1_ref[...], d2_ref[...], d3_ref[...])), axis=0, keepdims=True)
    below_ref[...] = jnp.sqrt(sums + 1e-06)


def lanes(parts):
    return parts[0] if len(parts) == 1 else jnp.concatenate(parts, axis=1)


def cut(v, n):
    return [v[:, k * PITCH : (k + 1) * PITCH] for k in range(n)]


def folded(v):
    total = v[:, :128]
    for k in range(1, v.shape[1] // 128):
        total = total + v[:, k * 128 : (k + 1) * 128]
    return total


def main(
    own_ref, row_one_ref, row_two_ref, col_one_ref, col_two_ref,
    w1_ref, w2_ref, w3_ref, w3t_ref, w2t_ref, w1t_ref, bias_ref,
    final_ref, grad_ref,
    xc0, xc1, wet_s, tgt, hm0, hm1, hc0, hc1, h2s, sp10, sp11, sp2, wd, em0, em1, e1s, rem, up, down, fin,
    b1g, b2g, b3g, g1, g2, g3, final_v, sem,
):
    below_ref, above_ref = by_side("gx", row_one_ref, row_two_ref)
    fromleft_ref, fromright_ref = by_side(GY, col_one_ref, col_two_ref)
    lane = lax.broadcasted_iota(jnp.int32, (8, 128), 1)
    zero = jnp.zeros((8, 128), F32)
    for r in range(-REACH, H + REACH):
        field, wet, target = row_parts(r, own_ref, below_ref, above_ref)
        at = (r + REACH) * 8
        block, by = divmod(r + REACH, 8)
        fl = fromleft_ref[block * 8 : block * 8 + 8, :]
        fr = fromright_ref[block * 8 : block * 8 + 8, :]

        def rim(first, width):
            right = turned(fr, -(by * 16 + first))
            left = turned(fl, -(by * 16 + first) - width)
            return jnp.where(lane < width, right, jnp.where(lane >= 128 - width, left, zero))

        row = jnp.concatenate([field, rim(0, 6)], axis=1)
        xc0[at * 3 : at * 3 + 24, :] = jnp.concatenate(
            [turned(row, 1), row, turned(row, -1)], axis=0
        )
        wet_s[at : at + 8, :] = jnp.concatenate([jnp.broadcast_to(wet, (8, W)), rim(6, 4)], axis=1)
        if target is not None:
            tgt[at : at + 8, :] = jnp.concatenate([target, rim(10, 2)], axis=1)
    for ref in (b1g, b2g, b3g, g1, g2, g3):
        ref[...] = jnp.zeros(ref.shape, F32)
    for r in (4, 5, 14, 15):
        em0[r * 64 : r * 64 + 64, :] = jnp.zeros((64, PITCH), BF)

    col = lax.broadcasted_iota(jnp.int32, (1, PITCH), 1)
    col = jnp.where(col < 320, col, col - PITCH) + lax.axis_index(GY) * W
    col_in = jnp.where((col >= 0) & (col < lax.axis_size(GY) * W), 1.0, 0.0).astype(F32)

    row0 = lax.axis_index("gx") * H

    def inside(r):
        i = row0 + r - REACH
        return col_in * jnp.where((i >= 0) & (i < lax.axis_size("gx") * H), 1.0, 0.0)

    def bias(at, n):
        b = bias_ref[at : at + n, :]
        return jnp.concatenate([b] * 3, axis=1)

    def part(ref, r, size, first=0, count=None):
        start = r * size + first
        return ref.at[start : start + (size if count is None else count), :]

    def loop(lo, hi, per, body):
        for first in range(lo, hi, per):
            body([first + REACH + k for k in range(per)])

    def thrice(v):
        return turned(v, 1), v, turned(v, -1)

    def conv(weights, ref, rs):
        y = dot(weights, lanes([part(ref, r - 1, 64, 0, 192)[...] for r in rs]))
        return [
            turned(v[0:64], 1) + v[64:128] + turned(v[128:192], -1) for v in cut(y, len(rs))
        ]

    def first_layer(xc, hm, hc, sp1):
        def body(rs):
            x9 = lanes([part(xc, r - 1, 24, 0, 72)[...].astype(BF) for r in rs])
            for r, z in zip(rs, cut(dot(w1_ref[...], x9), len(rs))):
                z = z + bias(0, 64)
                s = sigmoid(z)
                keep = inside(r)
                h = (z * s * keep).astype(BF)
                part(hm, r, 64)[...] = h
                if -1 <= r - REACH <= H:
                    for k, piece in enumerate(thrice(h)):
                        part(hc, r, 192, 64 * k, 64)[...] = piece
                    part(sp1, r, 64)[...] = silu_slope(z, s) * keep

        return body

    def second_layer(hm, rs):
        h2, slope = [], []
        for z in conv(w2_ref[...], hm, rs):
            z = z + bias(64, 64)
            s = sigmoid(z)
            h2.append((z * s).astype(BF))
            slope.append(silu_slope(z, s))
        q = cut(dot(w3_ref[...], lanes(h2)), len(rs))
        return lanes(h2), lanes(slope), lanes([sigmoid(v + bias(128, 32)) for v in q])

    def slopes(xc, r):
        x = part(xc, r, 24, 8, 8)[...]
        beside = (
            part(xc, r + 1, 24, 8, 8)[...],
            part(xc, r - 1, 24, 8, 8)[...],
            part(xc, r, 24, 16, 8)[...],
            part(xc, r, 24, 0, 8)[...],
        )
        return x, [b - x for b in beside]

    def tail_zero(rs):
        h2, slope, p = second_layer(hm0, rs)
        n = len(rs)
        for r, h2r, sr, pr in zip(rs, cut(h2, n), cut(slope, n), cut(p, n)):
            own = 0 <= r - REACH < H
            if own:
                part(h2s, r, 64)[...] = h2r
                part(sp2, r, 64)[...] = sr
            x, diff = slopes(xc0, r)
            wet = part(wet_s, r, 8)[...]
            change = jnp.zeros_like(x)
            for k in range(4):
                pk = pr[8 * k : 8 * k + 8]
                move = 0.25 * pk * diff[k]
                change = change + move
                if own:
                    part(wd, r, 32, 8 * k, 8)[...] = wet * move * (1.0 - pk)
            for k, piece in enumerate(thrice(x + wet * change)):
                part(xc1, r, 24, 8 * k, 8)[...] = piece

    def tail_grads(rs, e3, e2, h2, hc):
        b3g[...] += sum(folded(e[:, :W]) for e in e3)
        b2g[...] += sum(folded(e[:, :W]) for e in e2)
        g3[...] += dot_nt(
            lanes([e[:, :W].astype(BF) for e in e3]), lanes([v[:, :W] for v in h2])
        )
        g2[...] += dot_nt(
            lanes([part(hc, r - 1, 192, 0, 576)[:, :W] for r in rs]),
            lanes([e[:, :W].astype(BF) for e in e2]),
        )

    def of_block(rs, arrays):
        return [v for r, v in zip(rs, arrays) if 0 <= r - REACH < H]

    def tail_one(rs):
        h2, slope, p = second_layer(hm1, rs)
        n = len(rs)
        e3s = []
        for r, pr in zip(rs, cut(p, n)):
            x, diff = slopes(xc1, r)
            wet = part(wet_s, r, 8)[...]
            c = [0.25 * pr[8 * k : 8 * k + 8] for k in range(4)]
            move = [c[k] * diff[k] for k in range(4)]
            new = x + wet * (move[0] + move[1] + move[2] + move[3])
            if 0 <= r - REACH < H:
                part(fin, r, 8)[...] = new
            g = wet * (new - part(tgt, r, 8)[...])
            wg = wet * g
            t = [wg * c[k] for k in range(4)]
            left = g - t[0] - t[1] - t[2] - t[3]
            part(rem, r, 8)[...] = left + turned(t[2], 1) + turned(t[3], -1)
            part(up, r, 8)[...] = t[0]
            part(down, r, 8)[...] = t[1]
            e3s.append(
                jnp.concatenate(
                    [wg * move[k] * (1.0 - pr[8 * k : 8 * k + 8]) for k in range(4)], axis=0
                )
            )
        e2 = dot(w3t_ref[...], lanes([e.astype(BF) for e in e3s])) * slope
        e2s = cut(e2, n)
        for r, e in zip(rs, e2s):
            part(em1, r, 64)[...] = e.astype(BF)
        tail_grads(of_block(rs, rs), of_block(rs, e3s), of_block(rs, e2s), of_block(rs, cut(h2, n)), hc1)

    def first_error(em, sp1, rs):
        return [v * part(sp1, r, 64)[...] for r, v in zip(rs, conv(w2t_ref[...], em, rs))]

    def first_grads(rs, e1, xc, width):
        b1g[...] += sum(folded(e[:, :width]) for e in e1)
        g1[...] += dot_nt(
            lanes([e[:, :width].astype(BF) for e in e1]),
            lanes([part(xc, r - 1, 24, 0, 72)[:, :width].astype(BF) for r in rs]),
        )

    def first_one(rs):
        e1 = first_error(em1, sp11, rs)
        for r, e in zip(rs, e1):
            part(e1s, r, 64)[...] = e.astype(BF)
        first_grads(of_block(rs, rs), of_block(rs, e1), xc1, W)

    def back_zero(rs):
        y = dot(w1t_ref[...], lanes([part(e1s, r - 1, 64, 0, 192)[...] for r in rs]))
        e3s = []
        for r, yr in zip(rs, cut(y, len(rs))):
            g = part(rem, r, 8)[...] + part(up, r - 1, 8)[...] + part(down, r + 1, 8)[...]
            g = g + yr[8:16] + turned(yr[0:8], -1) + turned(yr[16:24], 1)
            e3 = jnp.concatenate([g] * 4, axis=0) * part(wd, r, 32)[...]
            e3s.append(jnp.concatenate([e3[:, :W], jnp.zeros((K, PITCH - W), F32)], axis=1))
        e2 = dot(w3t_ref[...], lanes([e.astype(BF) for e in e3s]))
        e2s = [v * part(sp2, r, 64)[...] for r, v in zip(rs, cut(e2, len(rs)))]
        for r, e in zip(rs, e2s):
            part(em0, r, 64)[...] = e.astype(BF)
        tail_grads(rs, e3s, e2s, [part(h2s, r, 64)[...] for r in rs], hc0)

    def first_zero(rs):
        first_grads(rs, first_error(em0, sp10, rs), xc0, PITCH)

    loop(-5, 13, 9, first_layer(xc0, hm0, hc0, sp10))
    loop(-4, 12, 16, tail_zero)
    loop(-3, 11, 14, first_layer(xc1, hm1, hc1, sp11))
    loop(-2, 10, 12, tail_one)
    for r in range(H):
        final_v[:, r, :] = fin[(r + REACH) * 8 : (r + REACH) * 8 + 8, :W]
    out = pltpu.make_async_copy(final_v, final_ref, sem)
    out.start()
    loop(-1, 9, 10, first_one)
    loop(0, 8, 8, back_zero)
    loop(-1, 9, 10, first_zero)

    grad_ref[0:256, :] = jnp.concatenate([g2[0:256, :], g2[256:512, :]], axis=1)
    grad_ref[256:320, :] = jnp.concatenate([g2[512:576, :], g1[:, 0:64]], axis=1)
    sums = [jnp.sum(ref[...], axis=1, keepdims=True) for ref in (b1g, b2g, b3g)]
    sums[2] = jnp.concatenate([sums[2], jnp.zeros((32, 1), F32)], axis=0)
    grad_ref[320:384, :] = jnp.concatenate(
        [
            g1[:, 64:72],
            *sums,
            jnp.zeros((64, 53), F32),
            jnp.concatenate([g3[...], jnp.zeros((32, 64), F32)], axis=0),
        ],
        axis=1,
    )
    out.wait()


def finish(total_ref, d1_ref, d2_ref, d3_ref, choose_ref, below_ref, u1_ref, u2_ref, u3_ref):
    t = [total_ref[k * 64 : k * 64 + 64, :] for k in range(6)]
    two = jnp.concatenate([v[:, :64].T for v in t[:4]] + [v[:, 64:].T for v in t[:4]] + [t[4][:, :64].T, t[5][:, 9:10]], axis=1)
    one = jnp.concatenate([t[4][:, 64:], t[5][:, :8], t[5][:, 8:9]], axis=1)
    three = jnp.concatenate([t[5][:32, 64:], t[5][:32, 10:11]], axis=1)
    grads = (one, two, three)
    squares = row_sums(grads)
    norm = jnp.sqrt(jnp.sum(squares, axis=0, keepdims=True))
    factor = 1.0 / jnp.maximum(norm, 1.0)
    clipped = [v * factor for v in grads]
    choose = choose_ref[...]
    ratios = factor * jnp.sqrt(jnp.sum(choose * squares, axis=0, keepdims=True)) / below_ref[...]
    row_ratio = jnp.sum(choose * ratios, axis=1, keepdims=True)
    scaling = math.sqrt(PARAMS)
    at = 0
    for ref, v, d_ref in zip((u1_ref, u2_ref, u3_ref), clipped, (d1_ref, d2_ref, d3_ref)):
        n = v.shape[0]
        ref[...] = scaling * (v + row_ratio[at : at + n] * d_ref[...])
        at += n


def shape(dims, dtype=F32):
    return jax.ShapeDtypeStruct(dims, dtype)


def kernel(body, outs, cost, mib, **more):
    return pl.pallas_call(
        body,
        out_shape=outs,
        cost_estimate=pl.CostEstimate(flops=cost, bytes_accessed=cost, transcendentals=0),
        compiler_params=pltpu.CompilerParams(vmem_limit_bytes=mib * 2**20),
        **more,
    )


def exchange(first, second, axis):
    count = lax.axis_size(axis)
    starts = (FIRST_SWAP[axis], 1 - FIRST_SWAP[axis])
    pairs = [[(i, i + 1) for i in range(start, count - 1, 2)] for start in starts]
    swaps = [[*p, *((b, a) for a, b in p)] for p in pairs]
    return lax.ppermute(first, axis, swaps[0]), lax.ppermute(second, axis, swaps[1])


def total_of(grad):
    near = ("gy_0", "gy_1")
    n = lax.axis_size(near)
    pieces = grad.reshape(n, -1, 128)
    own = jnp.sum(lax.all_to_all(pieces, near, 0, 0, tiled=True), axis=0)
    own = own + lax.ppermute(own, "gy_2", [(0, 1), (1, 0)])
    m = lax.axis_size("gx")
    copies = jnp.broadcast_to(own, (m, *own.shape))
    own = jnp.sum(lax.all_to_all(copies, "gx", 0, 0, tiled=True), axis=0)
    copies = jnp.broadcast_to(own, (n, *own.shape))
    return lax.all_to_all(copies, near, 0, 0, tiled=True).reshape(grad.shape)


def per_device(init, target, mask, one, two, head, d1, d2, d3, gid):
    hbm = pl.BlockSpec(memory_space=pltpu.HBM)
    vmem = pl.BlockSpec(memory_space=pltpu.VMEM)
    def widened(v, first):
        return jnp.pad(v, ((first, 2 * LEV + 1 - first - v.shape[0]), (0, 0), (0, 0)))

    own = widened(init, 0) + widened(target, LEV) + widened(mask[None], 2 * LEV).astype(F32)
    packs = kernel(pack_rows, [shape((72, W))] * 2, 10**5, 4)(own)
    rows_in = exchange(*packs, "gx")
    *weights, choose, below_ratio = kernel(
        prepare,
        [
            shape((C, 72), BF), shape((192, 192), BF), shape((K, C), BF), shape((C, K), BF),
            shape((192, 192), BF), shape((24, 192), BF), shape((160, 128)),
            shape((160, 128)), shape((1, 128)),
        ],
        10**6,
        8,
    )(one, two, head, d1, d2, d3, gid.reshape(1, -1))
    packs = kernel(pack_cols, [shape((24, 128))] * 2, 10**5, 4)(
        own, *rows_in, weights[6]
    )
    cols_in = exchange(*packs, GY)

    def rows(size, dtype=F32):
        return pltpu.VMEM((20 * size, PITCH), dtype)

    final, grad = kernel(
        main,
        [shape((LEV, H, W)), shape((384, 128))],
        10**7,
        40,
        in_specs=[vmem] * 12,
        out_specs=[hbm, vmem],
        scratch_shapes=[
            rows(24), rows(24), rows(8), rows(8), rows(64, BF), rows(64, BF), rows(192, BF), rows(192, BF), rows(64, BF),
            rows(64), rows(64), rows(64), rows(32), rows(64, BF), rows(64, BF), rows(64, BF),
            rows(8), rows(8), rows(8), rows(8),
            pltpu.VMEM((64, 128), F32), pltpu.VMEM((64, 128), F32), pltpu.VMEM((32, 128), F32),
            pltpu.VMEM((64, 72), F32), pltpu.VMEM((576, 64), F32), pltpu.VMEM((32, 64), F32),
            pltpu.VMEM((LEV, H, W), F32), pltpu.SemaphoreType.DMA,
        ],
    )(own, *rows_in, *cols_in, *weights)
    total = total_of(grad)
    u1, u2, u3 = kernel(finish, [shape(one.shape), shape(two.shape), shape(head.shape)], 10**6, 8)(
        total, d1, d2, d3, choose, below_ratio
    )
    return final, u1, u2, u3


def solution(mesh):
    count = mesh.shape["gy"] // 8
    torus = Mesh(mesh.devices.reshape(mesh.shape["gx"], count, 4, 2), ("gx", *GY))
    placed = (P(None, "gx", GY), P(None, "gx", GY), P("gx", GY), P(), P(), P(), P(), P(), P(), P())
    return jax.shard_map(
        per_device,
        mesh=torus,
        in_specs=placed,
        out_specs=(P(None, "gx", GY), P(), P(), P()),
        check_vma=False,
    )
```
